128 devices in a mesh: dp: 8 (over y_lo, z), cent: 16 (over x, y_hi, core).
Axes of the slice: x: 4, y: 4 (y_hi: 2, y_lo: 2; y = y_hi * 2 + y_lo), z: 4, core: 2. Of those that a mesh axis runs over, the one named last changes fastest.
Arguments:
- points: bfloat16 [524288, 1536], P(('dp', 'cent')), may hold values from -8 to 8
- assign: int32 [524288], P(('dp', 'cent')), may hold values from 0 to 2047, as said below
- counts: int32 [2048], P('cent'), may hold values from 1 to 1024, as said below
- level2: bfloat16 [256, 1536], P('cent'), may hold values from -3 to 3
- l2_assign: int32 [2048, 1], P('cent'), may hold values from 0 to 255, as said below
Outputs:
- new_level1: bfloat16 [2048, 1536], P('cent')
- nearest: float32 [2048], P('cent')
- new_level2: bfloat16 [256, 1536], P('cent')
The draws below stay inside these ranges and needn't reach their ends.
Inputs may be any that keep to these rules, and one draw needn't show every extreme that they name: `assign`: every level-1 centroid is named by at least one point; the points of each level-1 centroid stand in consecutive rows. counts[k] is the number of points of all devices whose assign is k. `l2_assign`: every level-2 centroid is named by at least one row; the owner of level-2 centroid j is j // 16; in each aligned block of 128 rows at most 16 rows name centroids of one owner, and some owner is named exactly that often in every block; the per-owner numbers of rows are, in every block, the same numbers in another order, and the centroids of each owner are named by exactly 128 rows in all.
All inputs are finite; a program needn't handle non-finite values.
Results may differ from the reference program's by a relative error of at most 0.013.
Values may be sent and summed in bfloat16 or wider, within the bound.
No kernel may reach another device: no remote copies, remote signals or barrier semaphores. Data moves between devices by JAX's collectives and lax.ppermute only.
A program may use at most 64 MiB of HBM per device.

```python
import jax
import jax.numpy as jnp
from jax import lax

D = 1536
PTS_DEV = 4096
K1_DEV = 128
K2_DEV = 16
PTS = 524288
K1 = 2048
K2 = 256
L2_CAP = 16
N_DP = 8
N_CENT = 16


def shared_assign(key):
    perm_key = jax.random.fold_in(key, 11)
    weight_key = jax.random.fold_in(key, 12)
    ordering = jax.random.permutation(perm_key, K1)
    busiest = 4 * (PTS // K1)
    weights = jax.random.randint(weight_key, (K1 - 2,), 1, 4).astype(jnp.int32)
    weight_total = jnp.sum(weights)
    cumulative = jnp.cumsum(weights).astype(jnp.int32)
    spare = PTS - busiest - 1 - (K1 - 2)
    bounds = spare // weight_total * cumulative + spare % weight_total * cumulative // weight_total
    shares = bounds - jnp.concatenate([jnp.zeros((1,), jnp.int32), bounds[:-1]])
    rest_counts = (1 + shares).astype(jnp.int32)
    all_counts = jnp.concatenate([jnp.full((1,), busiest, jnp.int32), jnp.ones((1,), jnp.int32), rest_counts])
    ends = jnp.cumsum(all_counts).astype(jnp.int32)
    positions = jnp.arange(PTS, dtype=jnp.int32)
    ranking = jnp.searchsorted(ends, positions, side='right').astype(jnp.int32)
    idents = ordering[ranking]
    return idents.astype(jnp.int32)


def draw_assign(key, part):
    idents = shared_assign(key)
    return idents


def draw_counts(key, part):
    idents = shared_assign(key)
    return jax.ops.segment_sum(jnp.ones((PTS,), jnp.int32), idents, num_segments=K1).astype(jnp.int32)


def draw_points(key, part):
    idents = shared_assign(key)
    key = jax.random.fold_in(key, 5)
    base_key = jax.random.fold_in(key, 1)
    noise_key = jax.random.fold_in(key, 2)
    centres = jnp.clip(jax.random.normal(base_key, (K1, D), jnp.float32), -4.0, 4.0)
    noise = jnp.clip(jax.random.normal(noise_key, (PTS, D), jnp.float32), -4.0, 4.0)
    return (centres[idents] + noise).astype(jnp.bfloat16)


def draw_l2_assign(key, part):
    key = jax.random.fold_in(key, 21)
    owner_total = N_CENT
    per_owner = K1_DEV // owner_total
    leftover = K1_DEV % owner_total
    slot_depth = L2_CAP
    positions = jnp.arange(owner_total, dtype=jnp.int32)
    even_fill = (per_owner + (positions < leftover).astype(jnp.int32)).astype(jnp.int32)
    taker_fill = even_fill[0::2]
    giver_fill = even_fill[1::2]
    headroom = jnp.minimum(giver_fill, slot_depth - taker_fill)
    transfer = jax.random.randint(jax.random.fold_in(key, 1), (owner_total // 2,), 0, headroom + 1).astype(jnp.int32)
    transfer = jnp.where(jnp.arange(owner_total // 2, dtype=jnp.int32) == 0, headroom, transfer)
    base_fill = jnp.stack([taker_fill + transfer, giver_fill - transfer], axis=1).reshape(owner_total)
    owner_perm = jax.random.permutation(jax.random.fold_in(key, 2), owner_total).astype(jnp.int32)
    block_shift = jax.random.permutation(jax.random.fold_in(key, 3), owner_total).astype(jnp.int32)
    fill_table = base_fill[(owner_perm[None, :] + block_shift[:, None]) % owner_total]
    fill_ends = jnp.cumsum(fill_table, axis=1).astype(jnp.int32)
    slot_index = jnp.arange(K1_DEV, dtype=jnp.int32)
    sorted_owner = jnp.sum((fill_ends[:, None, :] <= slot_index[None, :, None]).astype(jnp.int32), axis=2)
    shuffles = jax.vmap(lambda sub_key: jax.random.permutation(sub_key, K1_DEV))(jax.random.split(jax.random.fold_in(key, 4), owner_total))
    owner_ids = jnp.take_along_axis(sorted_owner, shuffles.astype(jnp.int32), axis=1).reshape(K1).astype(jnp.int32)
    ordering = jax.random.permutation(jax.random.fold_in(key, 5), K1).astype(jnp.int32)
    same_owner = owner_ids[:, None] == owner_ids[None, :]
    earlier = ordering[None, :] < ordering[:, None]
    slot_rank = jnp.sum((same_owner & earlier).astype(jnp.int32), axis=1)
    offsets = jax.random.randint(jax.random.fold_in(key, 6), (owner_total,), 0, K2_DEV).astype(jnp.int32)
    hottest = jax.random.randint(jax.random.fold_in(key, 7), (owner_total,), 0, K2_DEV).astype(jnp.int32)
    coin_flip = jax.random.randint(jax.random.fold_in(key, 8), (K1,), 0, 4).astype(jnp.int32)
    uniform_pick = jax.random.randint(jax.random.fold_in(key, 9), (K1,), 0, K2_DEV).astype(jnp.int32)
    rest_pick = jnp.where(coin_flip == 0, hottest[owner_ids], uniform_pick)
    local_ids = jnp.where(slot_rank < K2_DEV, (slot_rank + offsets[owner_ids]) % K2_DEV, rest_pick)
    return (owner_ids * K2_DEV + local_ids).astype(jnp.int32).reshape(K1, 1)


def shard_levels(own_key, shape, cuts, least, top_value):
    level, own = 1.0, jax.random.fold_in(own_key, 6)
    for position, shards_of in cuts:
        steps = jnp.exp(jax.random.uniform(jax.random.fold_in(own, position), (shards_of,), jnp.float32, least / len(cuts), top_value / len(cuts)))
        level = level * jnp.repeat(steps, shape[position] // shards_of).reshape([-1 if axis == position else 1 for axis in range(len(shape))])
    return level


def normal_values(key, extent, deviation, reach, shards=(), kind=jnp.bfloat16):
    entries = deviation * jax.random.normal(key, extent, jnp.float32)
    if shards:
        entries = entries * shard_levels(key, extent, shards, -0.22, 0.18)
    return jnp.clip(entries, -reach, reach).astype(kind)


def setup_inputs(seed: int = 0) -> dict:
    seeds = jax.random.split(jax.random.key(seed), 6)
    return {
        "points": draw_points(jax.random.fold_in(seeds[5], 71), 0),
        "assign": draw_assign(jax.random.fold_in(seeds[5], 71), 0),
        "counts": draw_counts(jax.random.fold_in(seeds[5], 71), 0),
        "level2": normal_values(seeds[3], (K2, D), 0.5, 3.0, ((0, 16),)),
        "l2_assign": draw_l2_assign(jax.random.fold_in(seeds[5], 71), 0),
    }


def reference(points, assign, counts, level2, l2_assign):
    device_count = N_DP * N_CENT
    point_blocks = points.reshape(device_count, PTS_DEV, D)
    ident_blocks = assign.reshape(device_count, PTS_DEV)

    def add_device(running, inputs):
        block, idents = inputs
        partial_sum = jax.ops.segment_sum(block.astype(jnp.float32), idents, num_segments=K1)
        rounded = lax.optimization_barrier(partial_sum.astype(jnp.bfloat16))
        return running + rounded.astype(jnp.float32), None

    sums_one, _ = lax.scan(add_device, jnp.zeros((K1, D), jnp.float32), (point_blocks, ident_blocks))
    new_level1 = (sums_one / counts.astype(jnp.float32)[:, None]).astype(jnp.bfloat16)

    as_float = new_level1.astype(jnp.float32)
    row_norms = jnp.sum(as_float * as_float, axis=1)
    centre_float = level2.astype(jnp.float32)
    centre_norms = jnp.sum(centre_float * centre_float, axis=1)
    cross = jnp.dot(new_level1, level2.T, preferred_element_type=jnp.float32)
    nearest = jnp.min((row_norms[:, None] - 2.0 * cross + centre_norms[None, :]) / D, axis=1)

    level2_labels = l2_assign[:, 0]
    sums_two = jax.ops.segment_sum(as_float, level2_labels, num_segments=K2)
    members_two = jax.ops.segment_sum(jnp.ones((K1,), jnp.float32), level2_labels, num_segments=K2)
    new_level2 = (sums_two / members_two[:, None]).astype(jnp.bfloat16)
    return new_level1, nearest, new_level2
```

```python
import jax
import jax.numpy as jnp
from jax import lax
from jax.experimental import pallas as pl
from jax.experimental.pallas import tpu as pltpu
from jax.sharding import PartitionSpec as P

BOTH = ("dp", "cent")
F32 = jnp.float32
BF16 = jnp.bfloat16
SLOTS = 32
LANES = 128
FIELDS = 16
COLS = 12
BLOCK = 512


def nt_dot(left, right):
    return lax.dot_general(left, right, (((1,), (1,)), ((), ())), preferred_element_type=F32)


def iota(shape, axis):
    return lax.broadcasted_iota(jnp.int32, shape, axis)


def run_sums_kernel(first_slot, *refs):
    if first_slot is None:
        slot_ref, *refs = refs
        first = slot_ref[0].astype(F32)
    else:
        first = float(first_slot)
    assign_ref, counts_ref, label_ref, points_ref, out_ref, rank_ref, acc_ref, id_ref, fields_ref, turned_ref = refs
    step = pl.program_id(0)
    rows_per = BLOCK // LANES
    steps = pl.num_programs(0)
    total_rows = assign_ref.shape[0]

    @pl.when(step == 0)
    def _():
        assign = assign_ref[...]
        row, lane = iota(assign.shape, 0), iota(assign.shape, 1)
        shifted = pltpu.roll(assign, 1, 1)
        before = jnp.where(lane == 0, pltpu.roll(shifted, 1, 0), shifted)
        starts = (assign != before) | ((row == 0) & (lane == 0))
        starts_f = jnp.where(starts, 1.0, 0.0)
        upper = jnp.where(iota((LANES, LANES), 0) <= iota((LANES, LANES), 1), 1.0, 0.0).astype(BF16)
        inner = jnp.dot(starts_f.astype(BF16), upper, preferred_element_type=F32)
        row_total = jnp.broadcast_to(inner[:, LANES - 1 :], inner.shape).astype(BF16)
        lower = jnp.where(iota((total_rows, total_rows), 1) < iota((total_rows, total_rows), 0), 1.0, 0.0)
        rank = inner + jnp.dot(lower.astype(BF16), row_total, preferred_element_type=F32) - 1.0
        rounds = (rank[total_rows - 1 :, LANES - 1 :].astype(jnp.int32) + SLOTS) // SLOTS
        rank = rank - first
        slot = iota((SLOTS, LANES), 0).astype(F32)
        named = jnp.where(starts, assign, 0).astype(F32)
        found = jnp.zeros((SLOTS, LANES), F32)
        for q in range(total_rows):
            rank_ref[q // rows_per, q % rows_per : q % rows_per + 1, :] = rank[q : q + 1, :]
            found = found + jnp.where(rank[q : q + 1, :] == slot, named[q : q + 1, :], 0.0)
        ids = jnp.broadcast_to(jnp.sum(found, axis=1, keepdims=True).astype(jnp.int32), (SLOTS, LANES))
        id_ref[...] = ids
        own = lax.axis_index("dp") * 16
        pick = iota((16, LANES), 1) == iota((16, LANES), 0) + own
        def picked(values):
            return jnp.broadcast_to(jnp.sum(jnp.where(pick, values, 0.0), axis=1, keepdims=True), (16, LANES))
        count = counts_ref[...]
        fields_ref[pl.ds(14, 16, stride=FIELDS), :] = picked(label_ref[...].astype(F32))
        fields_ref[pl.ds(14 + 16 * FIELDS, 16, stride=FIELDS), :] = picked((count // 256).astype(F32))
        fields_ref[pl.ds(15, 16, stride=FIELDS), :] = picked((count % 256).astype(F32))
        fields_ref[pl.ds(15 + 16 * FIELDS, 16, stride=FIELDS), :] = jnp.broadcast_to(rounds.astype(F32), (16, LANES))
        fields_ref[pl.ds(12, SLOTS, stride=FIELDS), :] = (ids // LANES).astype(F32)
        fields_ref[pl.ds(13, SLOTS, stride=FIELDS), :] = (ids % LANES).astype(F32)
        acc_ref[...] = jnp.zeros_like(acc_ref)

    slot = iota((SLOTS, LANES), 0).astype(F32)
    ranks = rank_ref[step]
    one_hot = jnp.concatenate(
        [jnp.where(ranks[q : q + 1, :] == slot, 1.0, 0.0).astype(BF16) for q in range(rows_per)], axis=1
    )
    acc_ref[...] += jnp.dot(one_hot, points_ref[...], preferred_element_type=F32)

    @pl.when(step == steps - 1)
    def _():
        for f in range(COLS):
            fields_ref[pl.ds(f, SLOTS, stride=FIELDS), :] = acc_ref[:, f * LANES : (f + 1) * LANES]
        for q in range(4):
            turned_ref[pl.ds(q, LANES, stride=4), :] = fields_ref[q * LANES : (q + 1) * LANES, :].T
        out_ref[...] = turned_ref[...].astype(BF16).reshape(LANES, 4, LANES)


def run_sums(points, assign, counts, labels, first_slot):
    rows, width = points.shape
    whole = lambda shape: pl.BlockSpec(shape, lambda i: (0,) * len(shape))
    static = isinstance(first_slot, int)
    specs = [
        whole((rows // LANES, LANES)),
        whole((1, LANES)),
        whole((1, LANES)),
        pl.BlockSpec((BLOCK, width), lambda i: (i, 0)),
    ]
    args = [assign, counts, labels, points]
    if not static:
        specs = [pl.BlockSpec(memory_space=pltpu.SMEM)] + specs
        args = [first_slot] + args

    def kernel(*refs):
        run_sums_kernel(first_slot if static else None, *refs)

    return pl.pallas_call(
        kernel,
        grid=(rows // BLOCK,),
        in_specs=specs,
        out_specs=whole((LANES, 4, LANES)),
        out_shape=jax.ShapeDtypeStruct((LANES, 4, LANES), BF16),
        scratch_shapes=[
            pltpu.VMEM((rows // BLOCK, BLOCK // LANES, LANES), F32),
            pltpu.VMEM((SLOTS, width), F32),
            pltpu.VMEM((SLOTS, LANES), jnp.int32),
            pltpu.VMEM((SLOTS * FIELDS, LANES), F32),
            pltpu.VMEM((SLOTS * FIELDS, LANES), F32),
        ],
        cost_estimate=pl.CostEstimate(
            flops=2 * 256 * rows * width, bytes_accessed=rows * width * 2, transcendentals=0
        ),
        compiler_params=pltpu.CompilerParams(vmem_limit_bytes=12 << 20),
        name="run_sums",
    )(*args)


def means_kernel(carried, *refs):
    if carried:
        runs_ref, before_ref, *refs = refs
    else:
        runs_ref, *refs = refs
    out_ref, acc_ref, rounds_ref, wide_ref, field_ref, send_ref = refs
    wide_ref[...] = runs_ref[...].reshape(4 * LANES, LANES).astype(F32)
    for q in range(4):
        field_ref[q * LANES : (q + 1) * LANES, :] = wide_ref[pl.ds(q, LANES, stride=4), :].T
    low_id = iota((LANES, LANES), 0).astype(F32)
    high_id = iota((16, LANES), 0).astype(F32)
    acc = before_ref[...] if carried else None
    for pair in range(SLOTS // 2):
        lefts, rights = [], []
        for r in (2 * pair, 2 * pair + 1):
            block = field_ref[r * FIELDS : (r + 1) * FIELDS, :]
            high = jnp.where(block[12:13, :] == high_id, 1.0, 0.0)
            rights.append(jnp.where(block[13:14, :] == low_id, 1.0, 0.0).astype(BF16))
            lefts.append(
                jnp.concatenate([(high[a : a + 1, :] * block).astype(BF16) for a in range(16)], axis=0)
            )
        part = nt_dot(jnp.concatenate(lefts, axis=1), jnp.concatenate(rights, axis=1))
        acc = part if acc is None else acc + part
    acc_ref[...] = acc

    device = iota((LANES, LANES), 1)
    same_dp = (device // 16) == (iota((LANES, LANES), 0) // 16)
    spread = []
    for first in (14, 14 + 16 * FIELDS, 15):
        value = field_ref[pl.ds(first, 16, stride=FIELDS), :]
        spread.append(jnp.where(same_dp, jnp.concatenate([value] * 8, axis=0), 0.0).astype(BF16))
    owner = jnp.where(iota((16, LANES), 1) % 16 == iota((16, LANES), 0), 1.0, 0.0).astype(BF16)
    numbers = nt_dot(owner, jnp.concatenate(spread, axis=0))
    label = numbers[:, :LANES].astype(jnp.int32)
    count = numbers[:, LANES : 2 * LANES] * 256.0 + numbers[:, 2 * LANES :]
    rounds = jnp.max(field_ref[15 + 16 * FIELDS : 16 + 16 * FIELDS, :])
    rounds_ref[0] = rounds.astype(jnp.int32)

    sums_two = jnp.zeros((16, COLS * 16), F32)
    members = jnp.zeros((16, 16), F32)
    for pair in range(8):
        owners, insides, values = [], [], []
        for a in (2 * pair, 2 * pair + 1):
            mean = (acc[a * 16 : (a + 1) * 16, :] / count[a : a + 1, :]).astype(BF16).astype(F32)
            send_ref[a * 16 : (a + 1) * 16, :] = mean
            own = label[a : a + 1, :]
            owners.append(jnp.where(own // 16 == iota((16, LANES), 0), 1.0, 0.0).astype(BF16))
            inside = jnp.where(own % 16 == iota((16, LANES), 0), 1.0, 0.0)
            insides.append(inside.astype(BF16))
            values.append(
                jnp.concatenate([(inside * mean[f : f + 1, :]).astype(BF16) for f in range(COLS)], axis=0)
            )
        left = jnp.concatenate(owners, axis=1)
        sums_two = sums_two + nt_dot(left, jnp.concatenate(values, axis=1))
        members = members + nt_dot(left, jnp.concatenate(insides, axis=1))
    repeat = jnp.where(iota((16, COLS * 16), 1) % 16 == iota((16, COLS * 16), 0), 1.0, 0.0).astype(BF16)
    members_wide = jnp.dot(members.astype(BF16), repeat, preferred_element_type=F32)
    level2 = sums_two / members_wide
    send_ref[pl.ds(12, 16, stride=16), :] = level2[:, :LANES]
    send_ref[pl.ds(13, 16, stride=16), :] = jnp.concatenate(
        [level2[:, LANES:], jnp.zeros((16, 2 * LANES - COLS * 16), F32)], axis=1
    )
    block = send_ref[...].astype(BF16).reshape(16, 16, LANES)
    for i in range(8):
        out_ref[i * 16 : (i + 1) * 16] = block


def means(runs, before=None):
    vmem = pl.BlockSpec(memory_space=pltpu.VMEM)
    args = [runs] if before is None else [runs, before]

    def kernel(*refs):
        means_kernel(before is not None, *refs)

    return pl.pallas_call(
        kernel,
        in_specs=[vmem] * len(args),
        out_specs=[vmem, vmem, pl.BlockSpec(memory_space=pltpu.SMEM)],
        out_shape=[
            jax.ShapeDtypeStruct((LANES, 16, LANES), BF16),
            jax.ShapeDtypeStruct((16 * FIELDS, LANES), F32),
            jax.ShapeDtypeStruct((1,), jnp.int32),
        ],
        scratch_shapes=[
            pltpu.VMEM((4 * LANES, LANES), F32),
            pltpu.VMEM((4 * LANES, LANES), F32),
            pltpu.VMEM((16 * FIELDS, LANES), F32),
        ],
        compiler_params=pltpu.CompilerParams(vmem_limit_bytes=8 << 20),
        name="means",
    )(*args)


def finish_kernel(parts, rows_ref, *refs):
    centre_refs, (level1_ref, nearest_ref, level2_ref, wide_ref) = refs[:parts], refs[parts:]
    wide_ref[...] = rows_ref[...].reshape(LANES * 16, LANES).astype(F32)
    width = COLS * LANES
    crosses = [None] * parts
    norm = jnp.zeros((1, LANES), F32)
    for f in range(COLS):
        columns = slice(f * LANES, (f + 1) * LANES)
        block = wide_ref[pl.ds(f, LANES, stride=16), :]
        level1_ref[:, columns] = block.T.astype(BF16)
        norm = norm + jnp.sum(block * block, axis=0, keepdims=True)
        small = block.astype(BF16)
        for p in range(parts):
            part = jnp.dot(centre_refs[p][:, columns], small, preferred_element_type=F32)
            crosses[p] = part if crosses[p] is None else crosses[p] + part
    best = None
    for p in range(parts):
        centre = centre_refs[p][...].astype(F32)
        centre_norm = jnp.sum(centre * centre, axis=1, keepdims=True)
        distance = (norm - 2.0 * crosses[p] + centre_norm) / width
        least = jnp.min(distance, axis=0, keepdims=True)
        best = least if best is None else jnp.minimum(best, least)
    nearest_ref[...] = best
    for half in range(2):
        block = wide_ref[pl.ds(12 + half, LANES, stride=16), :].T
        for f in range(8 * half, min(COLS, 8 * half + 8)):
            level2_ref[:, f * LANES : (f + 1) * LANES] = block[(f % 8) * 16 : (f % 8 + 1) * 16, :].astype(BF16)


def finish(rows, centres):
    vmem = pl.BlockSpec(memory_space=pltpu.VMEM)

    def kernel(*refs):
        finish_kernel(len(centres), *refs)

    return pl.pallas_call(
        kernel,
        in_specs=[vmem] * (1 + len(centres)),
        out_specs=[vmem] * 3,
        out_shape=[
            jax.ShapeDtypeStruct((LANES, COLS * LANES), BF16),
            jax.ShapeDtypeStruct((1, LANES), F32),
            jax.ShapeDtypeStruct((16, COLS * LANES), BF16),
        ],
        scratch_shapes=[pltpu.VMEM((LANES * 16, LANES), F32)],
        compiler_params=pltpu.CompilerParams(vmem_limit_bytes=8 << 20),
        name="finish",
    )(rows, *centres)


def exchange(value):
    return lax.all_to_all(value, BOTH, 0, 0, tiled=True)


def swapped(value, mask):
    return lax.ppermute(value, "cent", [(i, i ^ mask) for i in range(16)])


def body(points, assign, counts, level2, l2_assign):
    assign = assign.reshape(-1, LANES)
    counts = counts.reshape(1, LANES)
    labels = l2_assign.reshape(1, LANES)
    near = jnp.concatenate([level2] + [swapped(level2, mask) for mask in (1, 2, 3)], axis=0)
    sums = run_sums(points, assign, counts, labels, 0)
    centres = [near] + [swapped(near, mask) for mask in (4, 8, 12)]
    send, acc, rounds = means(exchange(sums))

    def more(state):
        index, _, acc = state
        sums = run_sums(points, assign, counts, labels, (index * SLOTS).reshape(1))
        send, acc, _ = means(exchange(sums), acc)
        return index + 1, send, acc

    _, send, _ = lax.while_loop(lambda state: state[0] < rounds[0], more, (jnp.int32(1), send, acc))
    new_level1, nearest, new_level2 = finish(exchange(send), centres)
    return new_level1, nearest.reshape(-1), new_level2


def solution(mesh):
    placed = (
        P(("dp", "cent"), None),
        P(("dp", "cent")),
        P("cent"),
        P("cent", None),
        P("cent", None),
    )
    return jax.shard_map(
        body,
        mesh=mesh,
        in_specs=placed,
        out_specs=(P("cent", None), P("cent"), P("cent", None)),
        check_vma=False,
    )
```

```python
import jax
import jax.numpy as jnp
from jax import lax
from jax.experimental import pallas as pl
from jax.experimental.pallas import tpu as pltpu
from jax.sharding import PartitionSpec as P

BOTH = ("dp", "cent")
F32 = jnp.float32
BF16 = jnp.bfloat16
SLOTS = 32
LANES = 128
FIELDS = 16
COLS = 12
BLOCK = 256


def nt_dot(left, right):
    return lax.dot_general(left, right, (((1,), (1,)), ((), ())), preferred_element_type=F32)


def iota(shape, axis):
    return lax.broadcasted_iota(jnp.int32, shape, axis)


def run_sums_kernel(first_slot, *refs):
    if first_slot is None:
        slot_ref, *refs = refs
        first = slot_ref[0].astype(F32)
    else:
        first = float(first_slot)
    assign_ref, counts_ref, label_ref, points_ref, out_ref, held_ref, fields_ref, turned_ref, arrived = refs
    total_rows = assign_ref.shape[0]
    blocks = points_ref.shape[0] // BLOCK
    copies = [
        pltpu.make_async_copy(
            points_ref.at[pl.ds(n * BLOCK, BLOCK)], held_ref.at[pl.ds(n * BLOCK, BLOCK)], arrived.at[n]
        )
        for n in range(blocks)
    ]
    for copy in copies:
        copy.start()

    assign = assign_ref[...]
    row, lane = iota(assign.shape, 0), iota(assign.shape, 1)
    shifted = pltpu.roll(assign, 1, 1)
    before = jnp.where(lane == 0, pltpu.roll(shifted, 1, 0), shifted)
    starts = (assign != before) | ((row == 0) & (lane == 0))
    upper = jnp.where(iota((LANES, LANES), 0) <= iota((LANES, LANES), 1), 1.0, 0.0).astype(BF16)
    inner = jnp.dot(jnp.where(starts, 1.0, 0.0).astype(BF16), upper, preferred_element_type=F32)
    row_total = jnp.broadcast_to(inner[:, LANES - 1 :], inner.shape).astype(BF16)
    lower = jnp.where(iota((total_rows, total_rows), 1) < iota((total_rows, total_rows), 0), 1.0, 0.0)
    rank = inner + jnp.dot(lower.astype(BF16), row_total, preferred_element_type=F32) - 1.0
    rounds = (rank[total_rows - 1 :, LANES - 1 :].astype(jnp.int32) + SLOTS) // SLOTS
    rank = rank - first
    slot = iota((SLOTS, LANES), 0).astype(F32)
    named = jnp.where(starts, assign, 0).astype(F32)
    found = jnp.zeros((SLOTS, LANES), F32)
    for q in range(total_rows):
        found = found + jnp.where(rank[q : q + 1, :] == slot, named[q : q + 1, :], 0.0)
    ids = jnp.broadcast_to(jnp.sum(found, axis=1, keepdims=True).astype(jnp.int32), (SLOTS, LANES))
    own = lax.axis_index("dp") * 16
    pick = iota((16, LANES), 1) == iota((16, LANES), 0) + own

    def picked(values):
        return jnp.broadcast_to(jnp.sum(jnp.where(pick, values, 0.0), axis=1, keepdims=True), (16, LANES))

    count = counts_ref[...]
    fields_ref[pl.ds(14, 16, stride=FIELDS), :] = picked(label_ref[...].astype(F32))
    fields_ref[pl.ds(14 + 16 * FIELDS, 16, stride=FIELDS), :] = picked((count // 256).astype(F32))
    fields_ref[pl.ds(15, 16, stride=FIELDS), :] = picked((count % 256).astype(F32))
    fields_ref[pl.ds(15 + 16 * FIELDS, 16, stride=FIELDS), :] = jnp.broadcast_to(rounds.astype(F32), (16, LANES))
    fields_ref[pl.ds(12, SLOTS, stride=FIELDS), :] = (ids // LANES).astype(F32)
    fields_ref[pl.ds(13, SLOTS, stride=FIELDS), :] = (ids % LANES).astype(F32)

    acc = None
    for n in range(blocks):
        copies[n].wait()
        rows = range(n * BLOCK // LANES, (n + 1) * BLOCK // LANES)
        one_hot = jnp.concatenate(
            [jnp.where(rank[q : q + 1, :] == slot, 1.0, 0.0).astype(BF16) for q in rows], axis=1
        )
        part = jnp.dot(one_hot, held_ref[n * BLOCK : (n + 1) * BLOCK, :], preferred_element_type=F32)
        acc = part if acc is None else acc + part
    for f in range(COLS):
        fields_ref[pl.ds(f, SLOTS, stride=FIELDS), :] = acc[:, f * LANES : (f + 1) * LANES]
    for q in range(4):
        turned_ref[pl.ds(q, LANES, stride=4), :] = fields_ref[q * LANES : (q + 1) * LANES, :].T
    out_ref[...] = turned_ref[...].astype(BF16).reshape(LANES, 4, LANES)


def run_sums(points, assign, counts, labels, first_slot):
    rows, width = points.shape
    vmem = pl.BlockSpec(memory_space=pltpu.VMEM)
    static = isinstance(first_slot, int)
    specs = [vmem, vmem, vmem, pl.BlockSpec(memory_space=pl.ANY)]
    args = [assign, counts, labels, points]
    if not static:
        specs = [pl.BlockSpec(memory_space=pltpu.SMEM)] + specs
        args = [first_slot] + args

    def kernel(*refs):
        run_sums_kernel(first_slot if static else None, *refs)

    return pl.pallas_call(
        kernel,
        in_specs=specs,
        out_specs=vmem,
        out_shape=jax.ShapeDtypeStruct((LANES, 4, LANES), BF16),
        scratch_shapes=[
            pltpu.VMEM((rows, width), BF16),
            pltpu.VMEM((SLOTS * FIELDS, LANES), F32),
            pltpu.VMEM((SLOTS * FIELDS, LANES), F32),
            pltpu.SemaphoreType.DMA((rows // BLOCK,)),
        ],
        cost_estimate=pl.CostEstimate(
            flops=2 * 256 * rows * width, bytes_accessed=rows * width * 2, transcendentals=0
        ),
        compiler_params=pltpu.CompilerParams(vmem_limit_bytes=20 << 20),
        name="run_sums",
    )(*args)


def means_kernel(carried, *refs):
    if carried:
        runs_ref, before_ref, *refs = refs
    else:
        runs_ref, *refs = refs
    out_ref, acc_ref, rounds_ref, wide_ref, field_ref, send_ref = refs
    wide_ref[...] = runs_ref[...].reshape(4 * LANES, LANES).astype(F32)
    for q in range(4):
        field_ref[q * LANES : (q + 1) * LANES, :] = wide_ref[pl.ds(q, LANES, stride=4), :].T
    low_id = iota((LANES, LANES), 0).astype(F32)
    high_id = iota((16, LANES), 0).astype(F32)
    acc = before_ref[...] if carried else None
    for pair in range(SLOTS // 2):
        lefts, rights = [], []
        for r in (2 * pair, 2 * pair + 1):
            block = field_ref[r * FIELDS : (r + 1) * FIELDS, :]
            high = jnp.where(block[12:13, :] == high_id, 1.0, 0.0)
            rights.append(jnp.where(block[13:14, :] == low_id, 1.0, 0.0).astype(BF16))
            lefts.append(
                jnp.concatenate([(high[a : a + 1, :] * block).astype(BF16) for a in range(16)], axis=0)
            )
        part = nt_dot(jnp.concatenate(lefts, axis=1), jnp.concatenate(rights, axis=1))
        acc = part if acc is None else acc + part
    acc_ref[...] = acc

    device = iota((LANES, LANES), 1)
    same_dp = (device // 16) == (iota((LANES, LANES), 0) // 16)
    spread = []
    for first in (14, 14 + 16 * FIELDS, 15):
        value = field_ref[pl.ds(first, 16, stride=FIELDS), :]
        spread.append(jnp.where(same_dp, jnp.concatenate([value] * 8, axis=0), 0.0).astype(BF16))
    owner = jnp.where(iota((16, LANES), 1) % 16 == iota((16, LANES), 0), 1.0, 0.0).astype(BF16)
    numbers = nt_dot(owner, jnp.concatenate(spread, axis=0))
    label = numbers[:, :LANES].astype(jnp.int32)
    count = numbers[:, LANES : 2 * LANES] * 256.0 + numbers[:, 2 * LANES :]
    rounds = jnp.max(field_ref[15 + 16 * FIELDS : 16 + 16 * FIELDS, :])
    rounds_ref[0] = rounds.astype(jnp.int32)

    sums_two = jnp.zeros((16, COLS * 16), F32)
    members = jnp.zeros((16, 16), F32)
    for pair in range(8):
        owners, insides, values = [], [], []
        for a in (2 * pair, 2 * pair + 1):
            mean = (acc[a * 16 : (a + 1) * 16, :] / count[a : a + 1, :]).astype(BF16).astype(F32)
            send_ref[a * 16 : (a + 1) * 16, :] = mean
            own = label[a : a + 1, :]
            owners.append(jnp.where(own // 16 == iota((16, LANES), 0), 1.0, 0.0).astype(BF16))
            inside = jnp.where(own % 16 == iota((16, LANES), 0), 1.0, 0.0)
            insides.append(inside.astype(BF16))
            values.append(
                jnp.concatenate([(inside * mean[f : f + 1, :]).astype(BF16) for f in range(COLS)], axis=0)
            )
        left = jnp.concatenate(owners, axis=1)
        sums_two = sums_two + nt_dot(left, jnp.concatenate(values, axis=1))
        members = members + nt_dot(left, jnp.concatenate(insides, axis=1))
    repeat = jnp.where(iota((16, COLS * 16), 1) % 16 == iota((16, COLS * 16), 0), 1.0, 0.0).astype(BF16)
    members_wide = jnp.dot(members.astype(BF16), repeat, preferred_element_type=F32)
    level2 = sums_two / members_wide
    send_ref[pl.ds(12, 16, stride=16), :] = level2[:, :LANES]
    send_ref[pl.ds(13, 16, stride=16), :] = jnp.concatenate(
        [level2[:, LANES:], jnp.zeros((16, 2 * LANES - COLS * 16), F32)], axis=1
    )
    block = send_ref[...].astype(BF16).reshape(16, 16, LANES)
    for i in range(8):
        out_ref[i * 16 : (i + 1) * 16] = block


def means(runs, before=None):
    vmem = pl.BlockSpec(memory_space=pltpu.VMEM)
    args = [runs] if before is None else [runs, before]

    def kernel(*refs):
        means_kernel(before is not None, *refs)

    return pl.pallas_call(
        kernel,
        in_specs=[vmem] * len(args),
        out_specs=[vmem, vmem, pl.BlockSpec(memory_space=pltpu.SMEM)],
        out_shape=[
            jax.ShapeDtypeStruct((LANES, 16, LANES), BF16),
            jax.ShapeDtypeStruct((16 * FIELDS, LANES), F32),
            jax.ShapeDtypeStruct((1,), jnp.int32),
        ],
        scratch_shapes=[
            pltpu.VMEM((4 * LANES, LANES), F32),
            pltpu.VMEM((4 * LANES, LANES), F32),
            pltpu.VMEM((16 * FIELDS, LANES), F32),
        ],
        compiler_params=pltpu.CompilerParams(vmem_limit_bytes=8 << 20),
        name="means",
    )(*args)


def finish_kernel(parts, rows_ref, *refs):
    centre_refs, (level1_ref, nearest_ref, level2_ref, wide_ref) = refs[:parts], refs[parts:]
    wide_ref[...] = rows_ref[...].reshape(LANES * 16, LANES).astype(F32)
    width = COLS * LANES
    crosses = [None] * parts
    norm = jnp.zeros((1, LANES), F32)
    for f in range(COLS):
        columns = slice(f * LANES, (f + 1) * LANES)
        block = wide_ref[pl.ds(f, LANES, stride=16), :]
        level1_ref[:, columns] = block.T.astype(BF16)
        norm = norm + jnp.sum(block * block, axis=0, keepdims=True)
        small = block.astype(BF16)
        for p in range(parts):
            part = jnp.dot(centre_refs[p][:, columns], small, preferred_element_type=F32)
            crosses[p] = part if crosses[p] is None else crosses[p] + part
    best = None
    for p in range(parts):
        centre = centre_refs[p][...].astype(F32)
        centre_norm = jnp.sum(centre * centre, axis=1, keepdims=True)
        distance = (norm - 2.0 * crosses[p] + centre_norm) / width
        least = jnp.min(distance, axis=0, keepdims=True)
        best = least if best is None else jnp.minimum(best, least)
    nearest_ref[...] = best
    for half in range(2):
        block = wide_ref[pl.ds(12 + half, LANES, stride=16), :].T
        for f in range(8 * half, min(COLS, 8 * half + 8)):
            level2_ref[:, f * LANES : (f + 1) * LANES] = block[(f % 8) * 16 : (f % 8 + 1) * 16, :].astype(BF16)


def finish(rows, centres):
    vmem = pl.BlockSpec(memory_space=pltpu.VMEM)

    def kernel(*refs):
        finish_kernel(len(centres), *refs)

    return pl.pallas_call(
        kernel,
        in_specs=[vmem] * (1 + len(centres)),
        out_specs=[vmem] * 3,
        out_shape=[
            jax.ShapeDtypeStruct((LANES, COLS * LANES), BF16),
            jax.ShapeDtypeStruct((1, LANES), F32),
            jax.ShapeDtypeStruct((16, COLS * LANES), BF16),
        ],
        scratch_shapes=[pltpu.VMEM((LANES * 16, LANES), F32)],
        compiler_params=pltpu.CompilerParams(vmem_limit_bytes=8 << 20),
        name="finish",
    )(rows, *centres)


def exchange(value):
    return lax.all_to_all(value, BOTH, 0, 0, tiled=True)


def swapped(value, mask):
    return lax.ppermute(value, "cent", [(i, i ^ mask) for i in range(16)])


def body(points, assign, counts, level2, l2_assign):
    assign = assign.reshape(-1, LANES)
    counts = counts.reshape(1, LANES)
    labels = l2_assign.reshape(1, LANES)
    near = jnp.concatenate([level2, swapped(level2, 2)], axis=0)
    sums, near = lax.optimization_barrier((run_sums(points, assign, counts, labels, 0), near))
    centres = jnp.concatenate([near] + [swapped(near, mask) for mask in (4, 8, 12)], axis=0)
    runs, centres = lax.optimization_barrier((exchange(sums), centres))
    centres = [centres, swapped(centres, 1)]
    send, acc, rounds = means(runs)

    def more(state):
        index, _, acc = state
        sums = run_sums(points, assign, counts, labels, (index * SLOTS).reshape(1))
        send, acc, _ = means(exchange(sums), acc)
        return index + 1, send, acc

    _, send, _ = lax.while_loop(lambda state: state[0] < rounds[0], more, (jnp.int32(1), send, acc))
    new_level1, nearest, new_level2 = finish(exchange(send), centres)
    return new_level1, nearest.reshape(-1), new_level2


def solution(mesh):
    placed = (
        P(("dp", "cent"), None),
        P(("dp", "cent")),
        P("cent"),
        P("cent", None),
        P("cent", None),
    )
    return jax.shard_map(
        body,
        mesh=mesh,
        in_specs=placed,
        out_specs=(P("cent", None), P("cent"), P("cent", None)),
        check_vma=False,
    )
```

```python
import jax
import jax.numpy as jnp
from jax import lax
from jax.experimental import pallas as pl
from jax.experimental.pallas import tpu as pltpu
from jax.sharding import PartitionSpec as P

BOTH = ("dp", "cent")
F32 = jnp.float32
BF16 = jnp.bfloat16
SLOTS = 32
LANES = 128
FIELDS = 16
COLS = 12
BLOCK = 256


def nt_dot(left, right):
    return lax.dot_general(left, right, (((1,), (1,)), ((), ())), preferred_element_type=F32)


def iota(shape, axis):
    return lax.broadcasted_iota(jnp.int32, shape, axis)


def run_sums_kernel(first_slot, *refs):
    if first_slot is None:
        slot_ref, *refs = refs
        first = slot_ref[0].astype(F32)
    else:
        first = float(first_slot)
    assign_hbm, counts_hbm, label_hbm, points_ref, out_ref, assign_ref, counts_ref, label_ref, held_ref, fields_ref, turned_ref, arrived, small = refs
    total_rows = assign_hbm.shape[0]
    blocks = points_ref.shape[0] // BLOCK
    copies = [
        pltpu.make_async_copy(
            points_ref.at[pl.ds(n * BLOCK, BLOCK)], held_ref.at[pl.ds(n * BLOCK, BLOCK)], arrived.at[n]
        )
        for n in range(blocks)
    ]
    numbers = [
        pltpu.make_async_copy(source, target, small.at[n])
        for n, (source, target) in enumerate(
            ((assign_hbm, assign_ref), (counts_hbm, counts_ref), (label_hbm, label_ref))
        )
    ]
    for copy in numbers:
        copy.start()
    for copy in copies:
        copy.start(priority=1)
    for copy in numbers:
        copy.wait()

    assign = assign_ref[...]
    row, lane = iota(assign.shape, 0), iota(assign.shape, 1)
    shifted = pltpu.roll(assign, 1, 1)
    before = jnp.where(lane == 0, pltpu.roll(shifted, 1, 0), shifted)
    starts = (assign != before) | ((row == 0) & (lane == 0))
    upper = jnp.where(iota((LANES, LANES), 0) <= iota((LANES, LANES), 1), 1.0, 0.0).astype(BF16)
    inner = jnp.dot(jnp.where(starts, 1.0, 0.0).astype(BF16), upper, preferred_element_type=F32)
    row_total = jnp.broadcast_to(inner[:, LANES - 1 :], inner.shape).astype(BF16)
    lower = jnp.where(iota((total_rows, total_rows), 1) < iota((total_rows, total_rows), 0), 1.0, 0.0)
    rank = inner + jnp.dot(lower.astype(BF16), row_total, preferred_element_type=F32) - 1.0
    rounds = (rank[total_rows - 1 :, LANES - 1 :].astype(jnp.int32) + SLOTS) // SLOTS
    rank = rank - first
    slot = iota((SLOTS, LANES), 0).astype(F32)
    named = jnp.where(starts, assign, 0).astype(F32)
    found = jnp.zeros((SLOTS, LANES), F32)
    for q in range(total_rows):
        found = found + jnp.where(rank[q : q + 1, :] == slot, named[q : q + 1, :], 0.0)
    ids = jnp.broadcast_to(jnp.sum(found, axis=1, keepdims=True).astype(jnp.int32), (SLOTS, LANES))
    own = lax.axis_index("dp") * 16
    pick = iota((16, LANES), 1) == iota((16, LANES), 0) + own

    def picked(values):
        return jnp.broadcast_to(jnp.sum(jnp.where(pick, values, 0.0), axis=1, keepdims=True), (16, LANES))

    count = counts_ref[...]
    fields_ref[pl.ds(14, 16, stride=FIELDS), :] = picked(label_ref[...].astype(F32))
    fields_ref[pl.ds(14 + 16 * FIELDS, 16, stride=FIELDS), :] = picked((count // 256).astype(F32))
    fields_ref[pl.ds(15, 16, stride=FIELDS), :] = picked((count % 256).astype(F32))
    fields_ref[pl.ds(15 + 16 * FIELDS, 16, stride=FIELDS), :] = jnp.broadcast_to(rounds.astype(F32), (16, LANES))
    fields_ref[pl.ds(12, SLOTS, stride=FIELDS), :] = (ids // LANES).astype(F32)
    fields_ref[pl.ds(13, SLOTS, stride=FIELDS), :] = (ids % LANES).astype(F32)

    acc = None
    for n in range(blocks):
        copies[n].wait()
        rows = range(n * BLOCK // LANES, (n + 1) * BLOCK // LANES)
        one_hot = jnp.concatenate(
            [jnp.where(rank[q : q + 1, :] == slot, 1.0, 0.0).astype(BF16) for q in rows], axis=1
        )
        part = jnp.dot(one_hot, held_ref[n * BLOCK : (n + 1) * BLOCK, :], preferred_element_type=F32)
        acc = part if acc is None else acc + part
    for f in range(COLS):
        fields_ref[pl.ds(f, SLOTS, stride=FIELDS), :] = acc[:, f * LANES : (f + 1) * LANES]
    for q in range(4):
        turned_ref[pl.ds(q, LANES, stride=4), :] = fields_ref[q * LANES : (q + 1) * LANES, :].T
    out_ref[...] = turned_ref[...].astype(BF16).reshape(LANES, 4, LANES)


def run_sums(points, assign, counts, labels, first_slot):
    rows, width = points.shape
    vmem = pl.BlockSpec(memory_space=pltpu.VMEM)
    static = isinstance(first_slot, int)
    specs = [pl.BlockSpec(memory_space=pl.ANY)] * 4
    args = [assign, counts, labels, points]
    if not static:
        specs = [pl.BlockSpec(memory_space=pltpu.SMEM)] + specs
        args = [first_slot] + args

    def kernel(*refs):
        run_sums_kernel(first_slot if static else None, *refs)

    return pl.pallas_call(
        kernel,
        in_specs=specs,
        out_specs=vmem,
        out_shape=jax.ShapeDtypeStruct((LANES, 4, LANES), BF16),
        scratch_shapes=[
            pltpu.VMEM(assign.shape, jnp.int32),
            pltpu.VMEM(counts.shape, jnp.int32),
            pltpu.VMEM(labels.shape, jnp.int32),
            pltpu.VMEM((rows, width), BF16),
            pltpu.VMEM((SLOTS * FIELDS, LANES), F32),
            pltpu.VMEM((SLOTS * FIELDS, LANES), F32),
            pltpu.SemaphoreType.DMA((rows // BLOCK,)),
            pltpu.SemaphoreType.DMA((3,)),
        ],
        cost_estimate=pl.CostEstimate(
            flops=2 * 256 * rows * width, bytes_accessed=rows * width * 2, transcendentals=0
        ),
        compiler_params=pltpu.CompilerParams(vmem_limit_bytes=20 << 20),
        name="run_sums",
    )(*args)


def means_kernel(carried, *refs):
    if carried:
        runs_ref, before_ref, *refs = refs
    else:
        runs_ref, *refs = refs
    out_ref, acc_ref, rounds_ref, wide_ref, field_ref, send_ref = refs
    wide_ref[...] = runs_ref[...].reshape(4 * LANES, LANES).astype(F32)
    for q in range(4):
        field_ref[q * LANES : (q + 1) * LANES, :] = wide_ref[pl.ds(q, LANES, stride=4), :].T
    low_id = iota((LANES, LANES), 0).astype(F32)
    high_id = iota((16, LANES), 0).astype(F32)
    acc = before_ref[...] if carried else None
    for pair in range(SLOTS // 2):
        lefts, rights = [], []
        for r in (2 * pair, 2 * pair + 1):
            block = field_ref[r * FIELDS : (r + 1) * FIELDS, :]
            high = jnp.where(block[12:13, :] == high_id, 1.0, 0.0)
            rights.append(jnp.where(block[13:14, :] == low_id, 1.0, 0.0).astype(BF16))
            lefts.append(
                jnp.concatenate([(high[a : a + 1, :] * block).astype(BF16) for a in range(16)], axis=0)
            )
        part = nt_dot(jnp.concatenate(lefts, axis=1), jnp.concatenate(rights, axis=1))
        acc = part if acc is None else acc + part
    acc_ref[...] = acc

    device = iota((LANES, LANES), 1)
    same_dp = (device // 16) == (iota((LANES, LANES), 0) // 16)
    spread = []
    for first in (14, 14 + 16 * FIELDS, 15):
        value = field_ref[pl.ds(first, 16, stride=FIELDS), :]
        spread.append(jnp.where(same_dp, jnp.concatenate([value] * 8, axis=0), 0.0).astype(BF16))
    owner = jnp.where(iota((16, LANES), 1) % 16 == iota((16, LANES), 0), 1.0, 0.0).astype(BF16)
    numbers = nt_dot(owner, jnp.concatenate(spread, axis=0))
    label = numbers[:, :LANES].astype(jnp.int32)
    count = numbers[:, LANES : 2 * LANES] * 256.0 + numbers[:, 2 * LANES :]
    rounds = jnp.max(field_ref[15 + 16 * FIELDS : 16 + 16 * FIELDS, :])
    rounds_ref[0] = rounds.astype(jnp.int32)

    sums_two = jnp.zeros((16, COLS * 16), F32)
    members = jnp.zeros((16, 16), F32)
    for pair in range(8):
        owners, insides, values = [], [], []
        for a in (2 * pair, 2 * pair + 1):
            mean = (acc[a * 16 : (a + 1) * 16, :] / count[a : a + 1, :]).astype(BF16).astype(F32)
            send_ref[a * 16 : (a + 1) * 16, :] = mean
            own = label[a : a + 1, :]
            owners.append(jnp.where(own // 16 == iota((16, LANES), 0), 1.0, 0.0).astype(BF16))
            inside = jnp.where(own % 16 == iota((16, LANES), 0), 1.0, 0.0)
            insides.append(inside.astype(BF16))
            values.append(
                jnp.concatenate([(inside * mean[f : f + 1, :]).astype(BF16) for f in range(COLS)], axis=0)
            )
        left = jnp.concatenate(owners, axis=1)
        sums_two = sums_two + nt_dot(left, jnp.concatenate(values, axis=1))
        members = members + nt_dot(left, jnp.concatenate(insides, axis=1))
    repeat = jnp.where(iota((16, COLS * 16), 1) % 16 == iota((16, COLS * 16), 0), 1.0, 0.0).astype(BF16)
    members_wide = jnp.dot(members.astype(BF16), repeat, preferred_element_type=F32)
    level2 = sums_two / members_wide
    send_ref[pl.ds(12, 16, stride=16), :] = level2[:, :LANES]
    send_ref[pl.ds(13, 16, stride=16), :] = jnp.concatenate(
        [level2[:, LANES:], jnp.zeros((16, 2 * LANES - COLS * 16), F32)], axis=1
    )
    block = send_ref[...].astype(BF16).reshape(16, 16, LANES)
    for i in range(8):
        out_ref[i * 16 : (i + 1) * 16] = block


def means(runs, before=None):
    vmem = pl.BlockSpec(memory_space=pltpu.VMEM)
    args = [runs] if before is None else [runs, before]

    def kernel(*refs):
        means_kernel(before is not None, *refs)

    return pl.pallas_call(
        kernel,
        in_specs=[vmem] * len(args),
        out_specs=[vmem, vmem, pl.BlockSpec(memory_space=pltpu.SMEM)],
        out_shape=[
            jax.ShapeDtypeStruct((LANES, 16, LANES), BF16),
            jax.ShapeDtypeStruct((16 * FIELDS, LANES), F32),
            jax.ShapeDtypeStruct((1,), jnp.int32),
        ],
        scratch_shapes=[
            pltpu.VMEM((4 * LANES, LANES), F32),
            pltpu.VMEM((4 * LANES, LANES), F32),
            pltpu.VMEM((16 * FIELDS, LANES), F32),
        ],
        compiler_params=pltpu.CompilerParams(vmem_limit_bytes=8 << 20),
        name="means",
    )(*args)


def finish_kernel(parts, rows_ref, *refs):
    centre_refs, (level1_ref, nearest_ref, level2_ref, wide_ref) = refs[:parts], refs[parts:]
    wide_ref[...] = rows_ref[...].reshape(LANES * 16, LANES).astype(F32)
    width = COLS * LANES
    crosses = [None] * parts
    norm = jnp.zeros((1, LANES), F32)
    for f in range(COLS):
        columns = slice(f * LANES, (f + 1) * LANES)
        block = wide_ref[pl.ds(f, LANES, stride=16), :]
        level1_ref[:, columns] = block.T.astype(BF16)
        norm = norm + jnp.sum(block * block, axis=0, keepdims=True)
        small = block.astype(BF16)
        for p in range(parts):
            part = jnp.dot(centre_refs[p][:, columns], small, preferred_element_type=F32)
            crosses[p] = part if crosses[p] is None else crosses[p] + part
    best = None
    for p in range(parts):
        centre = centre_refs[p][...].astype(F32)
        centre_norm = jnp.sum(centre * centre, axis=1, keepdims=True)
        distance = (norm - 2.0 * crosses[p] + centre_norm) / width
        least = jnp.min(distance, axis=0, keepdims=True)
        best = least if best is None else jnp.minimum(best, least)
    nearest_ref[...] = best
    for half in range(2):
        block = wide_ref[pl.ds(12 + half, LANES, stride=16), :].T
        for f in range(8 * half, min(COLS, 8 * half + 8)):
            level2_ref[:, f * LANES : (f + 1) * LANES] = block[(f % 8) * 16 : (f % 8 + 1) * 16, :].astype(BF16)


def finish(rows, centres):
    vmem = pl.BlockSpec(memory_space=pltpu.VMEM)

    def kernel(*refs):
        finish_kernel(len(centres), *refs)

    return pl.pallas_call(
        kernel,
        in_specs=[vmem] * (1 + len(centres)),
        out_specs=[vmem] * 3,
        out_shape=[
            jax.ShapeDtypeStruct((LANES, COLS * LANES), BF16),
            jax.ShapeDtypeStruct((1, LANES), F32),
            jax.ShapeDtypeStruct((16, COLS * LANES), BF16),
        ],
        scratch_shapes=[pltpu.VMEM((LANES * 16, LANES), F32)],
        compiler_params=pltpu.CompilerParams(vmem_limit_bytes=8 << 20),
        name="finish",
    )(rows, *centres)


def exchange(value):
    return lax.all_to_all(value, BOTH, 0, 0, tiled=True)


def swapped(value, mask):
    return lax.ppermute(value, "cent", [(i, i ^ mask) for i in range(16)])


def body(points, assign, counts, level2, l2_assign):
    assign = assign.reshape(-1, LANES)
    counts = counts.reshape(1, LANES)
    labels = l2_assign.reshape(1, LANES)
    sums, level2 = lax.optimization_barrier((run_sums(points, assign, counts, labels, 0), level2))
    near = jnp.concatenate([level2, swapped(level2, 2)], axis=0)
    runs = exchange(sums)
    centres = jnp.concatenate([near] + [swapped(near, mask) for mask in (4, 8, 12)], axis=0)
    send, acc, rounds = means(runs)
    send, centres = lax.optimization_barrier((send, centres))
    centres = [centres, swapped(centres, 1)]

    def more(state):
        index, _, acc = state
        sums = run_sums(points, assign, counts, labels, (index * SLOTS).reshape(1))
        send, acc, _ = means(exchange(sums), acc)
        return index + 1, send, acc

    _, send, _ = lax.while_loop(lambda state: state[0] < rounds[0], more, (jnp.int32(1), send, acc))
    new_level1, nearest, new_level2 = finish(exchange(send), centres)
    return new_level1, nearest.reshape(-1), new_level2


def solution(mesh):
    placed = (
        P(("dp", "cent"), None),
        P(("dp", "cent")),
        P("cent"),
        P("cent", None),
        P("cent", None),
    )
    return jax.shard_map(
        body,
        mesh=mesh,
        in_specs=placed,
        out_specs=(P("cent", None), P("cent"), P("cent", None)),
        check_vma=False,
    )
```

```python
import jax
import jax.numpy as jnp
from jax import lax
from jax.experimental import pallas as pl
from jax.experimental.pallas import tpu as pltpu
from jax.sharding import PartitionSpec as P

BOTH = ("dp", "cent")
F32 = jnp.float32
BF16 = jnp.bfloat16
SLOTS = 32
LANES = 128
FIELDS = 16
COLS = 12
BLOCK = 256


def nt_dot(left, right):
    return lax.dot_general(left, right, (((1,), (1,)), ((), ())), preferred_element_type=F32)


def iota(shape, axis):
    return lax.broadcasted_iota(jnp.int32, shape, axis)


def run_sums_kernel(first_slot, *refs):
    if first_slot is None:
        slot_ref, *refs = refs
        first = slot_ref[0].astype(F32)
    else:
        first = float(first_slot)
    assign_hbm, counts_hbm, label_hbm, points_ref, out_ref, assign_ref, counts_ref, label_ref, held_ref, fields_ref, turned_ref, arrived, small = refs
    total_rows = assign_hbm.shape[0]
    blocks = points_ref.shape[0] // BLOCK
    copies = [
        pltpu.make_async_copy(
            points_ref.at[pl.ds(n * BLOCK, BLOCK)], held_ref.at[pl.ds(n * BLOCK, BLOCK)], arrived.at[n]
        )
        for n in range(blocks)
    ]
    numbers = [
        pltpu.make_async_copy(source, target, small.at[n])
        for n, (source, target) in enumerate(
            ((assign_hbm, assign_ref), (counts_hbm, counts_ref), (label_hbm, label_ref))
        )
    ]
    for copy in numbers:
        copy.start()
    for copy in copies:
        copy.start(priority=1)
    for copy in numbers:
        copy.wait()

    assign = assign_ref[...]
    row, lane = iota(assign.shape, 0), iota(assign.shape, 1)
    shifted = pltpu.roll(assign, 1, 1)
    before = jnp.where(lane == 0, pltpu.roll(shifted, 1, 0), shifted)
    starts = (assign != before) | ((row == 0) & (lane == 0))
    upper = jnp.where(iota((LANES, LANES), 0) <= iota((LANES, LANES), 1), 1.0, 0.0).astype(BF16)
    inner = jnp.dot(jnp.where(starts, 1.0, 0.0).astype(BF16), upper, preferred_element_type=F32)
    row_total = jnp.broadcast_to(inner[:, LANES - 1 :], inner.shape).astype(BF16)
    lower = jnp.where(iota((total_rows, total_rows), 1) < iota((total_rows, total_rows), 0), 1.0, 0.0)
    rank = inner + jnp.dot(lower.astype(BF16), row_total, preferred_element_type=F32) - 1.0
    rounds = (rank[total_rows - 1 :, LANES - 1 :].astype(jnp.int32) + SLOTS) // SLOTS
    rank = rank - first
    slot = iota((SLOTS, LANES), 0).astype(F32)
    named = jnp.where(starts, assign, 0).astype(F32)
    found = jnp.zeros((SLOTS, LANES), F32)
    for q in range(total_rows):
        found = found + jnp.where(rank[q : q + 1, :] == slot, named[q : q + 1, :], 0.0)
    ids = jnp.broadcast_to(jnp.sum(found, axis=1, keepdims=True).astype(jnp.int32), (SLOTS, LANES))
    own = lax.axis_index("dp") * 16
    pick = iota((16, LANES), 1) == iota((16, LANES), 0) + own

    def picked(values):
        return jnp.broadcast_to(jnp.sum(jnp.where(pick, values, 0.0), axis=1, keepdims=True), (16, LANES))

    count = counts_ref[...]
    fields_ref[pl.ds(14, 16, stride=FIELDS), :] = picked(label_ref[...].astype(F32))
    fields_ref[pl.ds(14 + 16 * FIELDS, 16, stride=FIELDS), :] = picked((count // 256).astype(F32))
    fields_ref[pl.ds(15, 16, stride=FIELDS), :] = picked((count % 256).astype(F32))
    fields_ref[pl.ds(15 + 16 * FIELDS, 16, stride=FIELDS), :] = jnp.broadcast_to(rounds.astype(F32), (16, LANES))
    fields_ref[pl.ds(12, SLOTS, stride=FIELDS), :] = (ids // LANES).astype(F32)
    fields_ref[pl.ds(13, SLOTS, stride=FIELDS), :] = (ids % LANES).astype(F32)

    acc = None
    for n in range(blocks):
        copies[n].wait()
        rows = range(n * BLOCK // LANES, (n + 1) * BLOCK // LANES)
        one_hot = jnp.concatenate(
            [jnp.where(rank[q : q + 1, :] == slot, 1.0, 0.0).astype(BF16) for q in rows], axis=1
        )
        part = jnp.dot(one_hot, held_ref[n * BLOCK : (n + 1) * BLOCK, :], preferred_element_type=F32)
        acc = part if acc is None else acc + part
    for f in range(COLS):
        fields_ref[pl.ds(f, SLOTS, stride=FIELDS), :] = acc[:, f * LANES : (f + 1) * LANES]
    for q in range(4):
        turned_ref[pl.ds(q, LANES, stride=4), :] = fields_ref[q * LANES : (q + 1) * LANES, :].T
    out_ref[...] = turned_ref[...].astype(BF16).reshape(LANES, 4, LANES)


def run_sums(points, assign, counts, labels, first_slot):
    rows, width = points.shape
    vmem = pl.BlockSpec(memory_space=pltpu.VMEM)
    static = isinstance(first_slot, int)
    specs = [pl.BlockSpec(memory_space=pl.ANY)] * 4
    args = [assign, counts, labels, points]
    if not static:
        specs = [pl.BlockSpec(memory_space=pltpu.SMEM)] + specs
        args = [first_slot] + args

    def kernel(*refs):
        run_sums_kernel(first_slot if static else None, *refs)

    return pl.pallas_call(
        kernel,
        in_specs=specs,
        out_specs=vmem,
        out_shape=jax.ShapeDtypeStruct((LANES, 4, LANES), BF16),
        scratch_shapes=[
            pltpu.VMEM(assign.shape, jnp.int32),
            pltpu.VMEM(counts.shape, jnp.int32),
            pltpu.VMEM(labels.shape, jnp.int32),
            pltpu.VMEM((rows, width), BF16),
            pltpu.VMEM((SLOTS * FIELDS, LANES), F32),
            pltpu.VMEM((SLOTS * FIELDS, LANES), F32),
            pltpu.SemaphoreType.DMA((rows // BLOCK,)),
            pltpu.SemaphoreType.DMA((3,)),
        ],
        cost_estimate=pl.CostEstimate(
            flops=2 * 256 * rows * width, bytes_accessed=rows * width * 2, transcendentals=0
        ),
        compiler_params=pltpu.CompilerParams(vmem_limit_bytes=20 << 20),
        name="run_sums",
    )(*args)


def means_kernel(carried, *refs):
    if carried:
        runs_ref, before_ref, *refs = refs
    else:
        runs_ref, *refs = refs
    out_ref, acc_ref, rounds_ref, wide_ref, field_ref, send_ref = refs
    wide_ref[...] = runs_ref[...].reshape(4 * LANES, LANES).astype(F32)
    for q in range(4):
        field_ref[q * LANES : (q + 1) * LANES, :] = wide_ref[pl.ds(q, LANES, stride=4), :].T
    low_ids = [(iota((16, LANES), 0) + 16 * k).astype(BF16) for k in range(8)]
    one, zero = jnp.ones((16, LANES), BF16), jnp.zeros((16, LANES), BF16)

    def spread_row(ref, row):
        return jnp.broadcast_to(ref[row : row + 1, :], (16, LANES)).astype(BF16)

    acc = before_ref[...] if carried else None
    for pair in range(SLOTS // 2):
        lefts, rights = [], []
        for r in (2 * pair, 2 * pair + 1):
            block = field_ref[r * FIELDS : (r + 1) * FIELDS, :].astype(BF16)
            high = spread_row(field_ref, r * FIELDS + 12)
            low = spread_row(field_ref, r * FIELDS + 13)
            lefts.append(jnp.concatenate([jnp.where(high == a, block, zero) for a in range(16)], axis=0))
            rights.append(jnp.concatenate([jnp.where(low == ids, one, zero) for ids in low_ids], axis=0))
        part = nt_dot(jnp.concatenate(lefts, axis=1), jnp.concatenate(rights, axis=1))
        acc = part if acc is None else acc + part
    acc_ref[...] = acc

    device = iota((LANES, LANES), 1)
    same_dp = (device // 16) == (iota((LANES, LANES), 0) // 16)
    spread = []
    for first in (14, 14 + 16 * FIELDS, 15):
        value = field_ref[pl.ds(first, 16, stride=FIELDS), :]
        spread.append(jnp.where(same_dp, jnp.concatenate([value] * 8, axis=0), 0.0).astype(BF16))
    owner = jnp.where(iota((16, LANES), 1) % 16 == iota((16, LANES), 0), 1.0, 0.0).astype(BF16)
    numbers = nt_dot(owner, jnp.concatenate(spread, axis=0))
    label = numbers[:, :LANES].astype(jnp.int32)
    count = numbers[:, LANES : 2 * LANES] * 256.0 + numbers[:, 2 * LANES :]
    rounds = jnp.max(field_ref[15 + 16 * FIELDS : 16 + 16 * FIELDS, :])
    rounds_ref[0] = rounds.astype(jnp.int32)

    sums_two = None
    for pair in range(8):
        owners, values = [], []
        for a in (2 * pair, 2 * pair + 1):
            send_ref[a * 16 : (a + 1) * 16, :] = (
                (acc[a * 16 : (a + 1) * 16, :] / count[a : a + 1, :]).astype(BF16).astype(F32)
            )
            own = jnp.broadcast_to(label[a : a + 1, :], (16, LANES))
            owners.append(jnp.where(own // 16 == iota((16, LANES), 0), 1.0, 0.0).astype(BF16))
            inside = jnp.where(own % 16 == iota((16, LANES), 0), 1.0, 0.0).astype(BF16)
            values.append(
                jnp.concatenate(
                    [jnp.where(inside == one, spread_row(send_ref, a * 16 + f), zero) for f in range(COLS)]
                    + [inside],
                    axis=0,
                )
            )
        part = nt_dot(jnp.concatenate(values, axis=1), jnp.concatenate(owners, axis=1))
        sums_two = part if sums_two is None else sums_two + part
    members = sums_two[COLS * 16 :, :]
    level2 = jnp.concatenate([sums_two[f * 16 : (f + 1) * 16, :] / members for f in range(COLS)], axis=0).T
    send_ref[pl.ds(12, 16, stride=16), :] = level2[:, :LANES]
    send_ref[pl.ds(13, 16, stride=16), :] = jnp.concatenate(
        [level2[:, LANES:], jnp.zeros((16, 2 * LANES - COLS * 16), F32)], axis=1
    )
    block = send_ref[...].astype(BF16).reshape(16, 16, LANES)
    for i in range(8):
        out_ref[i * 16 : (i + 1) * 16] = block


def means(runs, before=None):
    vmem = pl.BlockSpec(memory_space=pltpu.VMEM)
    args = [runs] if before is None else [runs, before]

    def kernel(*refs):
        means_kernel(before is not None, *refs)

    return pl.pallas_call(
        kernel,
        in_specs=[vmem] * len(args),
        out_specs=[vmem, vmem, pl.BlockSpec(memory_space=pltpu.SMEM)],
        out_shape=[
            jax.ShapeDtypeStruct((LANES, 16, LANES), BF16),
            jax.ShapeDtypeStruct((16 * FIELDS, LANES), F32),
            jax.ShapeDtypeStruct((1,), jnp.int32),
        ],
        scratch_shapes=[
            pltpu.VMEM((4 * LANES, LANES), F32),
            pltpu.VMEM((4 * LANES, LANES), F32),
            pltpu.VMEM((16 * FIELDS, LANES), F32),
        ],
        compiler_params=pltpu.CompilerParams(vmem_limit_bytes=8 << 20),
        name="means",
    )(*args)


def finish_kernel(parts, rows_ref, *refs):
    centre_refs, (level1_ref, nearest_ref, level2_ref, wide_ref) = refs[:parts], refs[parts:]
    wide_ref[...] = rows_ref[...].reshape(LANES * 16, LANES).astype(F32)
    width = COLS * LANES
    crosses = [None] * parts
    norm = jnp.zeros((1, LANES), F32)
    for f in range(COLS):
        columns = slice(f * LANES, (f + 1) * LANES)
        block = wide_ref[pl.ds(f, LANES, stride=16), :]
        level1_ref[:, columns] = block.T.astype(BF16)
        norm = norm + jnp.sum(block * block, axis=0, keepdims=True)
        small = block.astype(BF16)
        for p in range(parts):
            part = jnp.dot(centre_refs[p][:, columns], small, preferred_element_type=F32)
            crosses[p] = part if crosses[p] is None else crosses[p] + part
    best = None
    for p in range(parts):
        centre = centre_refs[p][...].astype(F32)
        centre_norm = jnp.sum(centre * centre, axis=1, keepdims=True)
        distance = (norm - 2.0 * crosses[p] + centre_norm) / width
        least = jnp.min(distance, axis=0, keepdims=True)
        best = least if best is None else jnp.minimum(best, least)
    nearest_ref[...] = best
    for half in range(2):
        block = wide_ref[pl.ds(12 + half, LANES, stride=16), :].T
        for f in range(8 * half, min(COLS, 8 * half + 8)):
            level2_ref[:, f * LANES : (f + 1) * LANES] = block[(f % 8) * 16 : (f % 8 + 1) * 16, :].astype(BF16)


def finish(rows, centres):
    vmem = pl.BlockSpec(memory_space=pltpu.VMEM)

    def kernel(*refs):
        finish_kernel(len(centres), *refs)

    return pl.pallas_call(
        kernel,
        in_specs=[vmem] * (1 + len(centres)),
        out_specs=[vmem] * 3,
        out_shape=[
            jax.ShapeDtypeStruct((LANES, COLS * LANES), BF16),
            jax.ShapeDtypeStruct((1, LANES), F32),
            jax.ShapeDtypeStruct((16, COLS * LANES), BF16),
        ],
        scratch_shapes=[pltpu.VMEM((LANES * 16, LANES), F32)],
        compiler_params=pltpu.CompilerParams(vmem_limit_bytes=8 << 20),
        name="finish",
    )(rows, *centres)


def exchange(value):
    return lax.all_to_all(value, BOTH, 0, 0, tiled=True)


def swapped(value, mask):
    return lax.ppermute(value, "cent", [(i, i ^ mask) for i in range(16)])


def shifted(value, step):
    return lax.ppermute(value, "cent", [(i, (i + step) % 16) for i in range(16)])


def body(points, assign, counts, level2, l2_assign):
    assign = assign.reshape(-1, LANES)
    counts = counts.reshape(1, LANES)
    labels = l2_assign.reshape(1, LANES)
    sums, level2 = lax.optimization_barrier((run_sums(points, assign, counts, labels, 0), level2))
    near = jnp.concatenate([level2, swapped(level2, 2)], axis=0)
    runs = exchange(sums)
    centres = jnp.concatenate([near] + [swapped(near, mask) for mask in (4, 8, 12)], axis=0)
    send, acc, rounds = means(runs)
    centres = [centres, swapped(centres, 1)]

    def more(state):
        index, _, acc = state
        sums = run_sums(points, assign, counts, labels, (index * SLOTS).reshape(1))
        send, acc, _ = means(exchange(sums), acc)
        return index + 1, send, acc

    _, send, _ = lax.while_loop(lambda state: state[0] < rounds[0], more, (jnp.int32(1), send, acc))
    new_level1, nearest, new_level2 = finish(exchange(send), centres)
    return new_level1, nearest.reshape(-1), new_level2


def solution(mesh):
    placed = (
        P(("dp", "cent"), None),
        P(("dp", "cent")),
        P("cent"),
        P("cent", None),
        P("cent", None),
    )
    return jax.shard_map(
        body,
        mesh=mesh,
        in_specs=placed,
        out_specs=(P("cent", None), P("cent"), P("cent", None)),
        check_vma=False,
    )
```

```python
import jax
import jax.numpy as jnp
from jax import lax
from jax.experimental import pallas as pl
from jax.experimental.pallas import tpu as pltpu
from jax.sharding import PartitionSpec as P

BOTH = ("dp", "cent")
F32 = jnp.float32
BF16 = jnp.bfloat16
SLOTS = 32
LANES = 128
FIELDS = 16
COLS = 12
HALF = 7
BLOCK = 256


def nt_dot(left, right):
    return lax.dot_general(left, right, (((1,), (1,)), ((), ())), preferred_element_type=F32)


def iota(shape, axis):
    return lax.broadcasted_iota(jnp.int32, shape, axis)


def run_sums_kernel(first_slot, *refs):
    if first_slot is None:
        slot_ref, *refs = refs
        first = slot_ref[0].astype(F32)
    else:
        first = float(first_slot)
    assign_hbm, counts_hbm, label_hbm, points_ref, out_ref, assign_ref, counts_ref, label_ref, held_ref, fields_ref, turned_ref, arrived, small = refs
    total_rows = assign_hbm.shape[0]
    blocks = points_ref.shape[0] // BLOCK
    copies = [
        pltpu.make_async_copy(
            points_ref.at[pl.ds(n * BLOCK, BLOCK)], held_ref.at[pl.ds(n * BLOCK, BLOCK)], arrived.at[n]
        )
        for n in range(blocks)
    ]
    numbers = [
        pltpu.make_async_copy(source, target, small.at[n])
        for n, (source, target) in enumerate(
            ((assign_hbm, assign_ref), (counts_hbm, counts_ref), (label_hbm, label_ref))
        )
    ]
    for copy in numbers:
        copy.start()
    for copy in copies:
        copy.start(priority=1)
    for copy in numbers:
        copy.wait()

    assign = assign_ref[...]
    row, lane = iota(assign.shape, 0), iota(assign.shape, 1)
    shifted = pltpu.roll(assign, 1, 1)
    before = jnp.where(lane == 0, pltpu.roll(shifted, 1, 0), shifted)
    starts = (assign != before) | ((row == 0) & (lane == 0))
    upper = jnp.where(iota((LANES, LANES), 0) <= iota((LANES, LANES), 1), 1.0, 0.0).astype(BF16)
    inner = jnp.dot(jnp.where(starts, 1.0, 0.0).astype(BF16), upper, preferred_element_type=F32)
    row_total = jnp.broadcast_to(inner[:, LANES - 1 :], inner.shape).astype(BF16)
    lower = jnp.where(iota((total_rows, total_rows), 1) < iota((total_rows, total_rows), 0), 1.0, 0.0)
    rank = inner + jnp.dot(lower.astype(BF16), row_total, preferred_element_type=F32) - 1.0
    rounds = (rank[total_rows - 1 :, LANES - 1 :].astype(jnp.int32) + SLOTS) // SLOTS
    rank = rank - first
    slot = iota((SLOTS, LANES), 0).astype(F32)
    named = jnp.where(starts, assign, 0).astype(F32)
    found = jnp.zeros((SLOTS, LANES), F32)
    for q in range(total_rows):
        found = found + jnp.where(rank[q : q + 1, :] == slot, named[q : q + 1, :], 0.0)
    ids = jnp.broadcast_to(jnp.sum(found, axis=1, keepdims=True).astype(jnp.int32), (SLOTS, LANES))
    own = lax.axis_index("dp") * 16
    pick = iota((16, LANES), 1) == iota((16, LANES), 0) + own

    def picked(values):
        return jnp.broadcast_to(jnp.sum(jnp.where(pick, values, 0.0), axis=1, keepdims=True), (16, LANES))

    count = counts_ref[...]
    fields_ref[pl.ds(14, 16, stride=FIELDS), :] = picked(label_ref[...].astype(F32))
    fields_ref[pl.ds(14 + 16 * FIELDS, 16, stride=FIELDS), :] = picked((count // 256).astype(F32))
    fields_ref[pl.ds(15, 16, stride=FIELDS), :] = picked((count % 256).astype(F32))
    fields_ref[pl.ds(15 + 16 * FIELDS, 16, stride=FIELDS), :] = jnp.broadcast_to(rounds.astype(F32), (16, LANES))
    fields_ref[pl.ds(12, SLOTS, stride=FIELDS), :] = (ids // LANES).astype(F32)
    fields_ref[pl.ds(13, SLOTS, stride=FIELDS), :] = (ids % LANES).astype(F32)

    acc = None
    for n in range(blocks):
        copies[n].wait()
        rows = range(n * BLOCK // LANES, (n + 1) * BLOCK // LANES)
        one_hot = jnp.concatenate(
            [jnp.where(rank[q : q + 1, :] == slot, 1.0, 0.0).astype(BF16) for q in rows], axis=1
        )
        part = jnp.dot(one_hot, held_ref[n * BLOCK : (n + 1) * BLOCK, :], preferred_element_type=F32)
        acc = part if acc is None else acc + part
    for f in range(COLS):
        fields_ref[pl.ds(f, SLOTS, stride=FIELDS), :] = acc[:, f * LANES : (f + 1) * LANES]
    for q in range(4):
        turned_ref[pl.ds(q, LANES, stride=4), :] = fields_ref[q * LANES : (q + 1) * LANES, :].T
    out_ref[...] = turned_ref[...].astype(BF16).reshape(LANES, 4, LANES)


def run_sums(points, assign, counts, labels, first_slot):
    rows, width = points.shape
    vmem = pl.BlockSpec(memory_space=pltpu.VMEM)
    static = isinstance(first_slot, int)
    specs = [pl.BlockSpec(memory_space=pl.ANY)] * 4
    args = [assign, counts, labels, points]
    if not static:
        specs = [pl.BlockSpec(memory_space=pltpu.SMEM)] + specs
        args = [first_slot] + args

    def kernel(*refs):
        run_sums_kernel(first_slot if static else None, *refs)

    return pl.pallas_call(
        kernel,
        in_specs=specs,
        out_specs=vmem,
        out_shape=jax.ShapeDtypeStruct((LANES, 4, LANES), BF16),
        scratch_shapes=[
            pltpu.VMEM(assign.shape, jnp.int32),
            pltpu.VMEM(counts.shape, jnp.int32),
            pltpu.VMEM(labels.shape, jnp.int32),
            pltpu.VMEM((rows, width), BF16),
            pltpu.VMEM((SLOTS * FIELDS, LANES), F32),
            pltpu.VMEM((SLOTS * FIELDS, LANES), F32),
            pltpu.SemaphoreType.DMA((rows // BLOCK,)),
            pltpu.SemaphoreType.DMA((3,)),
        ],
        cost_estimate=pl.CostEstimate(
            flops=2 * 256 * rows * width, bytes_accessed=rows * width * 2, transcendentals=0
        ),
        compiler_params=pltpu.CompilerParams(vmem_limit_bytes=20 << 20),
        name="run_sums",
    )(*args)


def means_kernel(carried, *refs):
    if carried:
        runs_ref, before_ref, *refs = refs
    else:
        runs_ref, *refs = refs
    out_ref, acc_ref, rounds_ref, wide_ref, field_ref, send_ref, dense_ref = refs
    wide_ref[...] = runs_ref[...].reshape(4 * LANES, LANES).astype(F32)
    for q in range(4):
        field_ref[q * LANES : (q + 1) * LANES, :] = wide_ref[pl.ds(q, LANES, stride=4), :].T
    low_ids = [(iota((16, LANES), 0) + 16 * k).astype(BF16) for k in range(8)]
    one, zero = jnp.ones((16, LANES), BF16), jnp.zeros((16, LANES), BF16)

    def spread_row(ref, row):
        return jnp.broadcast_to(ref[row : row + 1, :], (16, LANES)).astype(BF16)

    acc = before_ref[...] if carried else None
    for pair in range(SLOTS // 2):
        lefts, rights = [], []
        for r in (2 * pair, 2 * pair + 1):
            block = field_ref[r * FIELDS : (r + 1) * FIELDS, :].astype(BF16)
            high = spread_row(field_ref, r * FIELDS + 12)
            low = spread_row(field_ref, r * FIELDS + 13)
            lefts.append(jnp.concatenate([jnp.where(high == a, block, zero) for a in range(16)], axis=0))
            rights.append(jnp.concatenate([jnp.where(low == ids, one, zero) for ids in low_ids], axis=0))
        part = nt_dot(jnp.concatenate(lefts, axis=1), jnp.concatenate(rights, axis=1))
        acc = part if acc is None else acc + part
    acc_ref[...] = acc

    device = iota((LANES, LANES), 1)
    same_dp = (device // 16) == (iota((LANES, LANES), 0) // 16)
    spread = []
    for first in (14, 14 + 16 * FIELDS, 15):
        value = field_ref[pl.ds(first, 16, stride=FIELDS), :]
        spread.append(jnp.where(same_dp, jnp.concatenate([value] * 8, axis=0), 0.0).astype(BF16))
    owner = jnp.where(iota((16, LANES), 1) % 16 == iota((16, LANES), 0), 1.0, 0.0).astype(BF16)
    numbers = nt_dot(owner, jnp.concatenate(spread, axis=0))
    label = numbers[:, :LANES].astype(jnp.int32)
    count = numbers[:, LANES : 2 * LANES] * 256.0 + numbers[:, 2 * LANES :]
    rounds = jnp.max(field_ref[15 + 16 * FIELDS : 16 + 16 * FIELDS, :])
    rounds_ref[0] = rounds.astype(jnp.int32)

    sums_two = None
    for pair in range(8):
        owners, values = [], []
        for a in (2 * pair, 2 * pair + 1):
            send_ref[a * 16 : (a + 1) * 16, :] = (
                (acc[a * 16 : (a + 1) * 16, :] / count[a : a + 1, :]).astype(BF16).astype(F32)
            )
            own = jnp.broadcast_to(label[a : a + 1, :], (16, LANES))
            owners.append(jnp.where(own // 16 == iota((16, LANES), 0), 1.0, 0.0).astype(BF16))
            inside = jnp.where(own % 16 == iota((16, LANES), 0), 1.0, 0.0).astype(BF16)
            values.append(
                jnp.concatenate(
                    [jnp.where(inside == one, spread_row(send_ref, a * 16 + f), zero) for f in range(COLS)]
                    + [inside],
                    axis=0,
                )
            )
        part = nt_dot(jnp.concatenate(values, axis=1), jnp.concatenate(owners, axis=1))
        sums_two = part if sums_two is None else sums_two + part
    members = sums_two[COLS * 16 :, :]
    level2 = jnp.concatenate([sums_two[f * 16 : (f + 1) * 16, :] / members for f in range(COLS)], axis=0).T
    send_ref[pl.ds(12, 16, stride=16), :] = level2[:, :LANES]
    send_ref[pl.ds(13, 16, stride=16), :] = jnp.concatenate(
        [level2[:, LANES:], jnp.zeros((16, 2 * LANES - COLS * 16), F32)], axis=1
    )
    for t in range(2 * HALF):
        half, place = t // HALF, t % HALF
        dense_ref[place, pl.ds(half, 16, stride=2), :] = send_ref[pl.ds(t, 16, stride=16), :]
    dense = jnp.concatenate([dense_ref[place] for place in range(HALF)], axis=1)
    block = dense.astype(BF16).reshape(16, 2, HALF * LANES)
    for i in range(8):
        out_ref[i * 16 : (i + 1) * 16] = block


def means(runs, before=None):
    vmem = pl.BlockSpec(memory_space=pltpu.VMEM)
    args = [runs] if before is None else [runs, before]

    def kernel(*refs):
        means_kernel(before is not None, *refs)

    return pl.pallas_call(
        kernel,
        in_specs=[vmem] * len(args),
        out_specs=[vmem, vmem, pl.BlockSpec(memory_space=pltpu.SMEM)],
        out_shape=[
            jax.ShapeDtypeStruct((LANES, 2, HALF * LANES), BF16),
            jax.ShapeDtypeStruct((16 * FIELDS, LANES), F32),
            jax.ShapeDtypeStruct((1,), jnp.int32),
        ],
        scratch_shapes=[
            pltpu.VMEM((4 * LANES, LANES), F32),
            pltpu.VMEM((4 * LANES, LANES), F32),
            pltpu.VMEM((16 * FIELDS, LANES), F32),
            pltpu.VMEM((HALF, 32, LANES), F32),
        ],
        compiler_params=pltpu.CompilerParams(vmem_limit_bytes=8 << 20),
        name="means",
    )(*args)


def finish_kernel(parts, rows_ref, *refs):
    centre_refs, (level1_ref, nearest_ref, level2_ref, wide_ref) = refs[:parts], refs[parts:]
    rows = rows_ref[...].reshape(2 * LANES, HALF * LANES).astype(F32)
    for place in range(HALF):
        wide_ref[place] = rows[:, place * LANES : (place + 1) * LANES]

    def taken(t):
        return wide_ref[t % HALF, pl.ds(t // HALF, LANES, stride=2), :]

    width = COLS * LANES
    crosses = [None] * parts
    norm = jnp.zeros((1, LANES), F32)
    for f in range(COLS):
        columns = slice(f * LANES, (f + 1) * LANES)
        block = taken(f)
        level1_ref[:, columns] = block.T.astype(BF16)
        norm = norm + jnp.sum(block * block, axis=0, keepdims=True)
        small = block.astype(BF16)
        for p in range(parts):
            part = jnp.dot(centre_refs[p][:, columns], small, preferred_element_type=F32)
            crosses[p] = part if crosses[p] is None else crosses[p] + part
    best = None
    for p in range(parts):
        centre = centre_refs[p][...].astype(F32)
        centre_norm = jnp.sum(centre * centre, axis=1, keepdims=True)
        distance = (norm - 2.0 * crosses[p] + centre_norm) / width
        least = jnp.min(distance, axis=0, keepdims=True)
        best = least if best is None else jnp.minimum(best, least)
    nearest_ref[...] = best
    for half in range(2):
        block = taken(12 + half).T
        for f in range(8 * half, min(COLS, 8 * half + 8)):
            level2_ref[:, f * LANES : (f + 1) * LANES] = block[(f % 8) * 16 : (f % 8 + 1) * 16, :].astype(BF16)


def finish(rows, centres):
    vmem = pl.BlockSpec(memory_space=pltpu.VMEM)

    def kernel(*refs):
        finish_kernel(len(centres), *refs)

    return pl.pallas_call(
        kernel,
        in_specs=[vmem] * (1 + len(centres)),
        out_specs=[vmem] * 3,
        out_shape=[
            jax.ShapeDtypeStruct((LANES, COLS * LANES), BF16),
            jax.ShapeDtypeStruct((1, LANES), F32),
            jax.ShapeDtypeStruct((16, COLS * LANES), BF16),
        ],
        scratch_shapes=[pltpu.VMEM((HALF, 2 * LANES, LANES), F32)],
        compiler_params=pltpu.CompilerParams(vmem_limit_bytes=8 << 20),
        name="finish",
    )(rows, *centres)


def exchange(value):
    return lax.all_to_all(value, BOTH, 0, 0, tiled=True)


def swapped(value, mask):
    return lax.ppermute(value, "cent", [(i, i ^ mask) for i in range(16)])


def shifted(value, step):
    return lax.ppermute(value, "cent", [(i, (i + step) % 16) for i in range(16)])


def body(points, assign, counts, level2, l2_assign):
    assign = assign.reshape(-1, LANES)
    counts = counts.reshape(1, LANES)
    labels = l2_assign.reshape(1, LANES)
    sums, level2 = lax.optimization_barrier((run_sums(points, assign, counts, labels, 0), level2))
    near = jnp.concatenate([level2, swapped(level2, 2)], axis=0)
    runs = exchange(sums)
    centres = jnp.concatenate([near] + [swapped(near, mask) for mask in (4, 8, 12)], axis=0)
    send, acc, rounds = means(runs)
    centres = [centres, swapped(centres, 1)]

    def more(state):
        index, _, acc = state
        sums = run_sums(points, assign, counts, labels, (index * SLOTS).reshape(1))
        send, acc, _ = means(exchange(sums), acc)
        return index + 1, send, acc

    _, send, _ = lax.while_loop(lambda state: state[0] < rounds[0], more, (jnp.int32(1), send, acc))
    new_level1, nearest, new_level2 = finish(exchange(send), centres)
    return new_level1, nearest.reshape(-1), new_level2


def solution(mesh):
    placed = (
        P(("dp", "cent"), None),
        P(("dp", "cent")),
        P("cent"),
        P("cent", None),
        P("cent", None),
    )
    return jax.shard_map(
        body,
        mesh=mesh,
        in_specs=placed,
        out_specs=(P("cent", None), P("cent"), P("cent", None)),
        check_vma=False,
    )
```

```python
import jax
import jax.numpy as jnp
from jax import lax
from jax.experimental import pallas as pl
from jax.experimental.pallas import tpu as pltpu
from jax.sharding import PartitionSpec as P

BOTH = ("dp", "cent")
F32 = jnp.float32
BF16 = jnp.bfloat16
SLOTS = 32
LANES = 128
FIELDS = 16
COLS = 12
HALF = 7
BLOCK = 256


def nt_dot(left, right):
    return lax.dot_general(left, right, (((1,), (1,)), ((), ())), preferred_element_type=F32)


def iota(shape, axis):
    return lax.broadcasted_iota(jnp.int32, shape, axis)


def run_sums_kernel(first_slot, *refs):
    if first_slot is None:
        slot_ref, *refs = refs
        first = slot_ref[0].astype(F32)
    else:
        first = float(first_slot)
    assign_hbm, counts_hbm, label_hbm, points_ref, out_ref, assign_ref, counts_ref, label_ref, held_ref, fields_ref, turned_ref, arrived, small = refs
    total_rows = assign_hbm.shape[0]
    blocks = points_ref.shape[0] // BLOCK
    copies = [
        pltpu.make_async_copy(
            points_ref.at[pl.ds(n * BLOCK, BLOCK)], held_ref.at[pl.ds(n * BLOCK, BLOCK)], arrived.at[n]
        )
        for n in range(blocks)
    ]
    numbers = [
        pltpu.make_async_copy(source, target, small.at[n])
        for n, (source, target) in enumerate(
            ((assign_hbm, assign_ref), (counts_hbm, counts_ref), (label_hbm, label_ref))
        )
    ]
    for copy in numbers:
        copy.start()
    for copy in copies:
        copy.start(priority=1)
    for copy in numbers:
        copy.wait()

    assign = assign_ref[...]
    row, lane = iota(assign.shape, 0), iota(assign.shape, 1)
    shifted = pltpu.roll(assign, 1, 1)
    before = jnp.where(lane == 0, pltpu.roll(shifted, 1, 0), shifted)
    starts = (assign != before) | ((row == 0) & (lane == 0))
    upper = jnp.where(iota((LANES, LANES), 0) <= iota((LANES, LANES), 1), 1.0, 0.0).astype(BF16)
    inner = jnp.dot(jnp.where(starts, 1.0, 0.0).astype(BF16), upper, preferred_element_type=F32)
    row_total = jnp.broadcast_to(inner[:, LANES - 1 :], inner.shape).astype(BF16)
    lower = jnp.where(iota((total_rows, total_rows), 1) < iota((total_rows, total_rows), 0), 1.0, 0.0)
    rank = inner + jnp.dot(lower.astype(BF16), row_total, preferred_element_type=F32) - 1.0
    rounds = (rank[total_rows - 1 :, LANES - 1 :].astype(jnp.int32) + SLOTS) // SLOTS
    rank = rank - first
    slot = iota((SLOTS, LANES), 0).astype(F32)
    named = jnp.where(starts, assign, 0).astype(F32)
    found = jnp.zeros((SLOTS, LANES), F32)
    for q in range(total_rows):
        found = found + jnp.where(rank[q : q + 1, :] == slot, named[q : q + 1, :], 0.0)
    ids = jnp.broadcast_to(jnp.sum(found, axis=1, keepdims=True).astype(jnp.int32), (SLOTS, LANES))
    own = lax.axis_index("dp") * 16
    pick = iota((16, LANES), 1) == iota((16, LANES), 0) + own

    def picked(values):
        return jnp.broadcast_to(jnp.sum(jnp.where(pick, values, 0.0), axis=1, keepdims=True), (16, LANES))

    count = counts_ref[...]
    fields_ref[pl.ds(14, 16, stride=FIELDS), :] = picked(label_ref[...].astype(F32))
    fields_ref[pl.ds(14 + 16 * FIELDS, 16, stride=FIELDS), :] = picked((count // 256).astype(F32))
    fields_ref[pl.ds(15, 16, stride=FIELDS), :] = picked((count % 256).astype(F32))
    fields_ref[pl.ds(15 + 16 * FIELDS, 16, stride=FIELDS), :] = jnp.broadcast_to(rounds.astype(F32), (16, LANES))
    fields_ref[pl.ds(12, SLOTS, stride=FIELDS), :] = (ids // LANES).astype(F32)
    fields_ref[pl.ds(13, SLOTS, stride=FIELDS), :] = (ids % LANES).astype(F32)

    acc = None
    for n in range(blocks):
        copies[n].wait()
        rows = range(n * BLOCK // LANES, (n + 1) * BLOCK // LANES)
        one_hot = jnp.concatenate(
            [jnp.where(rank[q : q + 1, :] == slot, 1.0, 0.0).astype(BF16) for q in rows], axis=1
        )
        part = jnp.dot(one_hot, held_ref[n * BLOCK : (n + 1) * BLOCK, :], preferred_element_type=F32)
        acc = part if acc is None else acc + part
    for f in range(COLS):
        fields_ref[pl.ds(f, SLOTS, stride=FIELDS), :] = acc[:, f * LANES : (f + 1) * LANES]
    for q in range(4):
        turned_ref[pl.ds(q, LANES, stride=4), :] = fields_ref[q * LANES : (q + 1) * LANES, :].T
    out_ref[...] = turned_ref[...].astype(BF16).reshape(LANES, 4, LANES)


def run_sums(points, assign, counts, labels, first_slot):
    rows, width = points.shape
    vmem = pl.BlockSpec(memory_space=pltpu.VMEM)
    static = isinstance(first_slot, int)
    specs = [pl.BlockSpec(memory_space=pl.ANY)] * 4
    args = [assign, counts, labels, points]
    if not static:
        specs = [pl.BlockSpec(memory_space=pltpu.SMEM)] + specs
        args = [first_slot] + args

    def kernel(*refs):
        run_sums_kernel(first_slot if static else None, *refs)

    return pl.pallas_call(
        kernel,
        in_specs=specs,
        out_specs=vmem,
        out_shape=jax.ShapeDtypeStruct((LANES, 4, LANES), BF16),
        scratch_shapes=[
            pltpu.VMEM(assign.shape, jnp.int32),
            pltpu.VMEM(counts.shape, jnp.int32),
            pltpu.VMEM(labels.shape, jnp.int32),
            pltpu.VMEM((rows, width), BF16),
            pltpu.VMEM((SLOTS * FIELDS, LANES), F32),
            pltpu.VMEM((SLOTS * FIELDS, LANES), F32),
            pltpu.SemaphoreType.DMA((rows // BLOCK,)),
            pltpu.SemaphoreType.DMA((3,)),
        ],
        cost_estimate=pl.CostEstimate(
            flops=2 * 256 * rows * width, bytes_accessed=rows * width * 2, transcendentals=0
        ),
        compiler_params=pltpu.CompilerParams(vmem_limit_bytes=20 << 20),
        name="run_sums",
    )(*args)


def means_kernel(carried, *refs):
    if carried:
        runs_ref, before_ref, *refs = refs
    else:
        runs_ref, *refs = refs
    out_ref, acc_ref, rounds_ref, wide_ref, field_ref, send_ref, dense_ref = refs
    wide_ref[...] = runs_ref[...].reshape(4 * LANES, LANES).astype(F32)
    for q in range(4):
        field_ref[q * LANES : (q + 1) * LANES, :] = wide_ref[pl.ds(q, LANES, stride=4), :].T
    low_ids = [(iota((16, LANES), 0) + 16 * k).astype(BF16) for k in range(8)]
    one, zero = jnp.ones((16, LANES), BF16), jnp.zeros((16, LANES), BF16)

    def spread_row(ref, row):
        return jnp.broadcast_to(ref[row : row + 1, :], (16, LANES)).astype(BF16)

    acc = before_ref[...] if carried else None
    for pair in range(SLOTS // 2):
        lefts, rights = [], []
        for r in (2 * pair, 2 * pair + 1):
            block = field_ref[r * FIELDS : (r + 1) * FIELDS, :].astype(BF16)
            high = spread_row(field_ref, r * FIELDS + 12)
            low = spread_row(field_ref, r * FIELDS + 13)
            lefts.append(jnp.concatenate([jnp.where(high == a, block, zero) for a in range(16)], axis=0))
            rights.append(jnp.concatenate([jnp.where(low == ids, one, zero) for ids in low_ids], axis=0))
        part = nt_dot(jnp.concatenate(lefts, axis=1), jnp.concatenate(rights, axis=1))
        acc = part if acc is None else acc + part
    acc_ref[...] = acc

    device = iota((LANES, LANES), 1)
    same_dp = (device // 16) == (iota((LANES, LANES), 0) // 16)
    spread = []
    for first in (14, 14 + 16 * FIELDS, 15):
        value = field_ref[pl.ds(first, 16, stride=FIELDS), :]
        spread.append(jnp.where(same_dp, jnp.concatenate([value] * 8, axis=0), 0.0).astype(BF16))
    owner = jnp.where(iota((16, LANES), 1) % 16 == iota((16, LANES), 0), 1.0, 0.0).astype(BF16)
    numbers = nt_dot(owner, jnp.concatenate(spread, axis=0))
    label = numbers[:, :LANES].astype(jnp.int32)
    count = numbers[:, LANES : 2 * LANES] * 256.0 + numbers[:, 2 * LANES :]
    rounds = jnp.max(field_ref[15 + 16 * FIELDS : 16 + 16 * FIELDS, :])
    rounds_ref[0] = rounds.astype(jnp.int32)

    sums_two = None
    for pair in range(8):
        owners, values = [], []
        for a in (2 * pair, 2 * pair + 1):
            send_ref[a * 16 : (a + 1) * 16, :] = (
                (acc[a * 16 : (a + 1) * 16, :] / count[a : a + 1, :]).astype(BF16).astype(F32)
            )
            own = jnp.broadcast_to(label[a : a + 1, :], (16, LANES))
            owners.append(jnp.where(own // 16 == iota((16, LANES), 0), 1.0, 0.0).astype(BF16))
            inside = jnp.where(own % 16 == iota((16, LANES), 0), 1.0, 0.0).astype(BF16)
            values.append(
                jnp.concatenate(
                    [jnp.where(inside == one, spread_row(send_ref, a * 16 + f), zero) for f in range(COLS)]
                    + [inside],
                    axis=0,
                )
            )
        part = nt_dot(jnp.concatenate(values, axis=1), jnp.concatenate(owners, axis=1))
        sums_two = part if sums_two is None else sums_two + part
    members = sums_two[COLS * 16 :, :]
    level2 = jnp.concatenate([sums_two[f * 16 : (f + 1) * 16, :] / members for f in range(COLS)], axis=0).T
    send_ref[pl.ds(12, 16, stride=16), :] = level2[:, :LANES]
    send_ref[pl.ds(13, 16, stride=16), :] = jnp.concatenate(
        [level2[:, LANES:], jnp.zeros((16, 2 * LANES - COLS * 16), F32)], axis=1
    )
    for t in range(2 * HALF):
        half, place = t // HALF, t % HALF
        dense_ref[place, pl.ds(half, 16, stride=2), :] = send_ref[pl.ds(t, 16, stride=16), :]
    dense = jnp.concatenate([dense_ref[place] for place in range(HALF)], axis=1)
    block = dense.astype(BF16).reshape(16, 2, HALF * LANES)
    for i in range(8):
        out_ref[i * 16 : (i + 1) * 16] = block


def means(runs, before=None):
    vmem = pl.BlockSpec(memory_space=pltpu.VMEM)
    args = [runs] if before is None else [runs, before]

    def kernel(*refs):
        means_kernel(before is not None, *refs)

    return pl.pallas_call(
        kernel,
        in_specs=[vmem] * len(args),
        out_specs=[vmem, vmem, pl.BlockSpec(memory_space=pltpu.SMEM)],
        out_shape=[
            jax.ShapeDtypeStruct((LANES, 2, HALF * LANES), BF16),
            jax.ShapeDtypeStruct((16 * FIELDS, LANES), F32),
            jax.ShapeDtypeStruct((1,), jnp.int32),
        ],
        scratch_shapes=[
            pltpu.VMEM((4 * LANES, LANES), F32),
            pltpu.VMEM((4 * LANES, LANES), F32),
            pltpu.VMEM((16 * FIELDS, LANES), F32),
            pltpu.VMEM((HALF, 32, LANES), F32),
        ],
        compiler_params=pltpu.CompilerParams(vmem_limit_bytes=8 << 20),
        name="means",
    )(*args)


def finish_kernel(parts, rows_ref, *refs):
    centre_refs, (level1_ref, nearest_ref, level2_ref, wide_ref) = refs[:parts], refs[parts:]
    rows = rows_ref[...].reshape(2 * LANES, HALF * LANES).astype(F32)
    for place in range(HALF):
        wide_ref[place] = rows[:, place * LANES : (place + 1) * LANES]

    def taken(t):
        return wide_ref[t % HALF, pl.ds(t // HALF, LANES, stride=2), :]

    width = COLS * LANES
    crosses = [None] * parts
    norm = jnp.zeros((1, LANES), F32)
    for f in range(COLS):
        columns = slice(f * LANES, (f + 1) * LANES)
        block = taken(f)
        level1_ref[:, columns] = block.T.astype(BF16)
        norm = norm + jnp.sum(block * block, axis=0, keepdims=True)
        small = block.astype(BF16)
        for p in range(parts):
            part = jnp.dot(centre_refs[p][:, columns], small, preferred_element_type=F32)
            crosses[p] = part if crosses[p] is None else crosses[p] + part
    best = None
    for p in range(parts):
        centre = centre_refs[p][...].astype(F32)
        centre_norm = jnp.sum(centre * centre, axis=1, keepdims=True)
        distance = (norm - 2.0 * crosses[p] + centre_norm) / width
        least = jnp.min(distance, axis=0, keepdims=True)
        best = least if best is None else jnp.minimum(best, least)
    nearest_ref[...] = best
    for half in range(2):
        block = taken(12 + half).T
        for f in range(8 * half, min(COLS, 8 * half + 8)):
            level2_ref[:, f * LANES : (f + 1) * LANES] = block[(f % 8) * 16 : (f % 8 + 1) * 16, :].astype(BF16)


def finish(rows, centres):
    vmem = pl.BlockSpec(memory_space=pltpu.VMEM)

    def kernel(*refs):
        finish_kernel(len(centres), *refs)

    return pl.pallas_call(
        kernel,
        in_specs=[vmem] * (1 + len(centres)),
        out_specs=[vmem] * 3,
        out_shape=[
            jax.ShapeDtypeStruct((LANES, COLS * LANES), BF16),
            jax.ShapeDtypeStruct((1, LANES), F32),
            jax.ShapeDtypeStruct((16, COLS * LANES), BF16),
        ],
        scratch_shapes=[pltpu.VMEM((HALF, 2 * LANES, LANES), F32)],
        compiler_params=pltpu.CompilerParams(vmem_limit_bytes=8 << 20),
        name="finish",
    )(rows, *centres)


def exchange(value):
    return lax.all_to_all(value, BOTH, 0, 0, tiled=True)


def swapped(value, mask):
    return lax.ppermute(value, "cent", [(i, i ^ mask) for i in range(16)])


def shifted(value, step):
    return lax.ppermute(value, "cent", [(i, (i + step) % 16) for i in range(16)])


def across(value):
    return lax.ppermute(value, BOTH, [(i, i ^ (4 * 16 + 2)) for i in range(128)])


def body(points, assign, counts, level2, l2_assign):
    assign = assign.reshape(-1, LANES)
    counts = counts.reshape(1, LANES)
    labels = l2_assign.reshape(1, LANES)
    sums, level2 = lax.optimization_barrier((run_sums(points, assign, counts, labels, 0), level2))
    near = jnp.concatenate([level2, across(level2)], axis=0)
    runs = exchange(sums)
    centres = jnp.concatenate([near] + [swapped(near, mask) for mask in (4, 8, 12)], axis=0)
    send, acc, rounds = means(runs)
    centres = [centres, swapped(centres, 1)]

    def more(state):
        index, _, acc = state
        sums = run_sums(points, assign, counts, labels, (index * SLOTS).reshape(1))
        send, acc, _ = means(exchange(sums), acc)
        return index + 1, send, acc

    _, send, _ = lax.while_loop(lambda state: state[0] < rounds[0], more, (jnp.int32(1), send, acc))
    new_level1, nearest, new_level2 = finish(exchange(send), centres)
    return new_level1, nearest.reshape(-1), new_level2


def solution(mesh):
    placed = (
        P(("dp", "cent"), None),
        P(("dp", "cent")),
        P("cent"),
        P("cent", None),
        P("cent", None),
    )
    return jax.shard_map(
        body,
        mesh=mesh,
        in_specs=placed,
        out_specs=(P("cent", None), P("cent"), P("cent", None)),
        check_vma=False,
    )
```

```python
import jax
import jax.numpy as jnp
from jax import lax
from jax.experimental import pallas as pl
from jax.experimental.pallas import tpu as pltpu
from jax.sharding import PartitionSpec as P

BOTH = ("dp", "cent")
F32 = jnp.float32
BF16 = jnp.bfloat16
SLOTS = 32
LANES = 128
FIELDS = 16
COLS = 12
HALF = 7
BLOCK = 256


def nt_dot(left, right):
    return lax.dot_general(left, right, (((1,), (1,)), ((), ())), preferred_element_type=F32)


def iota(shape, axis):
    return lax.broadcasted_iota(jnp.int32, shape, axis)


def run_sums_kernel(first_slot, *refs):
    if first_slot is None:
        slot_ref, *refs = refs
        first = slot_ref[0].astype(F32)
    else:
        first = float(first_slot)
    assign_hbm, counts_hbm, label_hbm, points_ref, out_ref, assign_ref, counts_ref, label_ref, held_ref, fields_ref, turned_ref, arrived, small = refs
    total_rows = assign_hbm.shape[0]
    blocks = points_ref.shape[0] // BLOCK
    copies = [
        pltpu.make_async_copy(
            points_ref.at[pl.ds(n * BLOCK, BLOCK)], held_ref.at[pl.ds(n * BLOCK, BLOCK)], arrived.at[n]
        )
        for n in range(blocks)
    ]
    numbers = [
        pltpu.make_async_copy(source, target, small.at[n])
        for n, (source, target) in enumerate(
            ((assign_hbm, assign_ref), (counts_hbm, counts_ref), (label_hbm, label_ref))
        )
    ]
    for copy in numbers:
        copy.start()
    for copy in copies:
        copy.start(priority=1)
    for copy in numbers:
        copy.wait()

    assign = assign_ref[...]
    row, lane = iota(assign.shape, 0), iota(assign.shape, 1)
    shifted = pltpu.roll(assign, 1, 1)
    before = jnp.where(lane == 0, pltpu.roll(shifted, 1, 0), shifted)
    starts = (assign != before) | ((row == 0) & (lane == 0))
    upper = jnp.where(iota((LANES, LANES), 0) <= iota((LANES, LANES), 1), 1.0, 0.0).astype(BF16)
    inner = jnp.dot(jnp.where(starts, 1.0, 0.0).astype(BF16), upper, preferred_element_type=F32)
    row_total = jnp.broadcast_to(inner[:, LANES - 1 :], inner.shape).astype(BF16)
    lower = jnp.where(iota((total_rows, total_rows), 1) < iota((total_rows, total_rows), 0), 1.0, 0.0)
    rank = inner + jnp.dot(lower.astype(BF16), row_total, preferred_element_type=F32) - 1.0
    rounds = (rank[total_rows - 1 :, LANES - 1 :].astype(jnp.int32) + SLOTS) // SLOTS
    rank = rank - first
    slot = iota((SLOTS, LANES), 0).astype(F32)
    named = jnp.where(starts, assign, 0).astype(F32)
    found = jnp.zeros((SLOTS, LANES), F32)
    for q in range(total_rows):
        found = found + jnp.where(rank[q : q + 1, :] == slot, named[q : q + 1, :], 0.0)
    ids = jnp.broadcast_to(jnp.sum(found, axis=1, keepdims=True).astype(jnp.int32), (SLOTS, LANES))
    own = lax.axis_index("dp") * 16
    pick = iota((16, LANES), 1) == iota((16, LANES), 0) + own

    def picked(values):
        return jnp.broadcast_to(jnp.sum(jnp.where(pick, values, 0.0), axis=1, keepdims=True), (16, LANES))

    count = counts_ref[...]
    fields_ref[pl.ds(14, 16, stride=FIELDS), :] = picked(label_ref[...].astype(F32))
    fields_ref[pl.ds(14 + 16 * FIELDS, 16, stride=FIELDS), :] = picked((count // 256).astype(F32))
    fields_ref[pl.ds(15, 16, stride=FIELDS), :] = picked((count % 256).astype(F32))
    fields_ref[pl.ds(15 + 16 * FIELDS, 16, stride=FIELDS), :] = jnp.broadcast_to(rounds.astype(F32), (16, LANES))
    fields_ref[pl.ds(12, SLOTS, stride=FIELDS), :] = (ids // LANES).astype(F32)
    fields_ref[pl.ds(13, SLOTS, stride=FIELDS), :] = (ids % LANES).astype(F32)

    acc = None
    for n in range(blocks):
        copies[n].wait()
        rows = range(n * BLOCK // LANES, (n + 1) * BLOCK // LANES)
        one_hot = jnp.concatenate(
            [jnp.where(rank[q : q + 1, :] == slot, 1.0, 0.0).astype(BF16) for q in rows], axis=1
        )
        part = jnp.dot(one_hot, held_ref[n * BLOCK : (n + 1) * BLOCK, :], preferred_element_type=F32)
        acc = part if acc is None else acc + part
    for f in range(COLS):
        fields_ref[pl.ds(f, SLOTS, stride=FIELDS), :] = acc[:, f * LANES : (f + 1) * LANES]
    for q in range(4):
        turned_ref[pl.ds(q, LANES, stride=4), :] = fields_ref[q * LANES : (q + 1) * LANES, :].T
    out_ref[...] = turned_ref[...].astype(BF16).reshape(LANES, 4, LANES)


def run_sums(points, assign, counts, labels, first_slot):
    rows, width = points.shape
    vmem = pl.BlockSpec(memory_space=pltpu.VMEM)
    static = isinstance(first_slot, int)
    specs = [pl.BlockSpec(memory_space=pl.ANY)] * 4
    args = [assign, counts, labels, points]
    if not static:
        specs = [pl.BlockSpec(memory_space=pltpu.SMEM)] + specs
        args = [first_slot] + args

    def kernel(*refs):
        run_sums_kernel(first_slot if static else None, *refs)

    return pl.pallas_call(
        kernel,
        in_specs=specs,
        out_specs=vmem,
        out_shape=jax.ShapeDtypeStruct((LANES, 4, LANES), BF16),
        scratch_shapes=[
            pltpu.VMEM(assign.shape, jnp.int32),
            pltpu.VMEM(counts.shape, jnp.int32),
            pltpu.VMEM(labels.shape, jnp.int32),
            pltpu.VMEM((rows, width), BF16),
            pltpu.VMEM((SLOTS * FIELDS, LANES), F32),
            pltpu.VMEM((SLOTS * FIELDS, LANES), F32),
            pltpu.SemaphoreType.DMA((rows // BLOCK,)),
            pltpu.SemaphoreType.DMA((3,)),
        ],
        cost_estimate=pl.CostEstimate(
            flops=2 * 256 * rows * width, bytes_accessed=rows * width * 2, transcendentals=0
        ),
        compiler_params=pltpu.CompilerParams(vmem_limit_bytes=20 << 20),
        name="run_sums",
    )(*args)


def means_kernel(carried, *refs):
    if carried:
        runs_ref, before_ref, *refs = refs
    else:
        runs_ref, *refs = refs
    out_ref, acc_ref, rounds_ref, wide_ref, field_ref, send_ref, dense_ref = refs
    wide_ref[...] = runs_ref[...].reshape(4 * LANES, LANES).astype(F32)
    for q in range(4):
        field_ref[q * LANES : (q + 1) * LANES, :] = wide_ref[pl.ds(q, LANES, stride=4), :].T
    low_ids = [(iota((16, LANES), 0) + 16 * k).astype(BF16) for k in range(8)]
    one, zero = jnp.ones((16, LANES), BF16), jnp.zeros((16, LANES), BF16)

    def spread_row(ref, row):
        return jnp.broadcast_to(ref[row : row + 1, :], (16, LANES)).astype(BF16)

    acc = before_ref[...] if carried else None
    for pair in range(SLOTS // 2):
        lefts, rights = [], []
        for r in (2 * pair, 2 * pair + 1):
            block = field_ref[r * FIELDS : (r + 1) * FIELDS, :].astype(BF16)
            high = spread_row(field_ref, r * FIELDS + 12)
            low = spread_row(field_ref, r * FIELDS + 13)
            lefts.append(jnp.concatenate([jnp.where(high == a, block, zero) for a in range(16)], axis=0))
            rights.append(jnp.concatenate([jnp.where(low == ids, one, zero) for ids in low_ids], axis=0))
        part = nt_dot(jnp.concatenate(lefts, axis=1), jnp.concatenate(rights, axis=1))
        acc = part if acc is None else acc + part
    acc_ref[...] = acc

    device = iota((LANES, LANES), 1)
    same_dp = (device // 16) == (iota((LANES, LANES), 0) // 16)
    spread = []
    for first in (14, 14 + 16 * FIELDS, 15):
        value = field_ref[pl.ds(first, 16, stride=FIELDS), :]
        spread.append(jnp.where(same_dp, jnp.concatenate([value] * 8, axis=0), 0.0).astype(BF16))
    owner = jnp.where(iota((16, LANES), 1) % 16 == iota((16, LANES), 0), 1.0, 0.0).astype(BF16)
    numbers = nt_dot(owner, jnp.concatenate(spread, axis=0))
    label = numbers[:, :LANES].astype(jnp.int32)
    count = numbers[:, LANES : 2 * LANES] * 256.0 + numbers[:, 2 * LANES :]
    rounds = jnp.max(field_ref[15 + 16 * FIELDS : 16 + 16 * FIELDS, :])
    rounds_ref[0] = rounds.astype(jnp.int32)

    sums_two = None
    for pair in range(8):
        owners, values = [], []
        for a in (2 * pair, 2 * pair + 1):
            send_ref[a * 16 : (a + 1) * 16, :] = (
                (acc[a * 16 : (a + 1) * 16, :] / count[a : a + 1, :]).astype(BF16).astype(F32)
            )
            own = jnp.broadcast_to(label[a : a + 1, :], (16, LANES))
            owners.append(jnp.where(own // 16 == iota((16, LANES), 0), 1.0, 0.0).astype(BF16))
            inside = jnp.where(own % 16 == iota((16, LANES), 0), 1.0, 0.0).astype(BF16)
            values.append(
                jnp.concatenate(
                    [jnp.where(inside == one, spread_row(send_ref, a * 16 + f), zero) for f in range(COLS)]
                    + [inside],
                    axis=0,
                )
            )
        part = nt_dot(jnp.concatenate(values, axis=1), jnp.concatenate(owners, axis=1))
        sums_two = part if sums_two is None else sums_two + part
    members = sums_two[COLS * 16 :, :]
    level2 = jnp.concatenate([sums_two[f * 16 : (f + 1) * 16, :] / members for f in range(COLS)], axis=0).T
    send_ref[pl.ds(12, 16, stride=16), :] = level2[:, :LANES]
    send_ref[pl.ds(13, 16, stride=16), :] = jnp.concatenate(
        [level2[:, LANES:], jnp.zeros((16, 2 * LANES - COLS * 16), F32)], axis=1
    )
    for t in range(2 * HALF):
        half, place = t // HALF, t % HALF
        dense_ref[place, pl.ds(half, 16, stride=2), :] = send_ref[pl.ds(t, 16, stride=16), :]
    dense = jnp.concatenate([dense_ref[place] for place in range(HALF)], axis=1)
    block = dense.astype(BF16).reshape(16, 2, HALF * LANES)
    for i in range(8):
        out_ref[i * 16 : (i + 1) * 16] = block


def means(runs, before=None):
    vmem = pl.BlockSpec(memory_space=pltpu.VMEM)
    args = [runs] if before is None else [runs, before]

    def kernel(*refs):
        means_kernel(before is not None, *refs)

    return pl.pallas_call(
        kernel,
        in_specs=[vmem] * len(args),
        out_specs=[vmem, vmem, pl.BlockSpec(memory_space=pltpu.SMEM)],
        out_shape=[
            jax.ShapeDtypeStruct((LANES, 2, HALF * LANES), BF16),
            jax.ShapeDtypeStruct((16 * FIELDS, LANES), F32),
            jax.ShapeDtypeStruct((1,), jnp.int32),
        ],
        scratch_shapes=[
            pltpu.VMEM((4 * LANES, LANES), F32),
            pltpu.VMEM((4 * LANES, LANES), F32),
            pltpu.VMEM((16 * FIELDS, LANES), F32),
            pltpu.VMEM((HALF, 32, LANES), F32),
        ],
        compiler_params=pltpu.CompilerParams(vmem_limit_bytes=8 << 20),
        name="means",
    )(*args)


def finish_kernel(parts, rows_ref, *refs):
    centre_refs, (level1_ref, nearest_ref, level2_ref, wide_ref) = refs[:parts], refs[parts:]
    rows = rows_ref[...].reshape(2 * LANES, HALF * LANES).astype(F32)
    for place in range(HALF):
        wide_ref[place] = rows[:, place * LANES : (place + 1) * LANES]

    def taken(t):
        return wide_ref[t % HALF, pl.ds(t // HALF, LANES, stride=2), :]

    width = COLS * LANES
    crosses = [None] * parts
    norm = jnp.zeros((1, LANES), F32)
    for f in range(COLS):
        columns = slice(f * LANES, (f + 1) * LANES)
        block = taken(f)
        level1_ref[:, columns] = block.T.astype(BF16)
        norm = norm + jnp.sum(block * block, axis=0, keepdims=True)
        small = block.astype(BF16)
        for p in range(parts):
            part = jnp.dot(centre_refs[p][:, columns], small, preferred_element_type=F32)
            crosses[p] = part if crosses[p] is None else crosses[p] + part
    best = None
    for p in range(parts):
        centre = centre_refs[p][...].astype(F32)
        centre_norm = jnp.sum(centre * centre, axis=1, keepdims=True)
        distance = (norm - 2.0 * crosses[p] + centre_norm) / width
        least = jnp.min(distance, axis=0, keepdims=True)
        best = least if best is None else jnp.minimum(best, least)
    nearest_ref[...] = best
    for half in range(2):
        block = taken(12 + half).T
        for f in range(8 * half, min(COLS, 8 * half + 8)):
            level2_ref[:, f * LANES : (f + 1) * LANES] = block[(f % 8) * 16 : (f % 8 + 1) * 16, :].astype(BF16)


def finish(rows, centres):
    vmem = pl.BlockSpec(memory_space=pltpu.VMEM)

    def kernel(*refs):
        finish_kernel(len(centres), *refs)

    return pl.pallas_call(
        kernel,
        in_specs=[vmem] * (1 + len(centres)),
        out_specs=[vmem] * 3,
        out_shape=[
            jax.ShapeDtypeStruct((LANES, COLS * LANES), BF16),
            jax.ShapeDtypeStruct((1, LANES), F32),
            jax.ShapeDtypeStruct((16, COLS * LANES), BF16),
        ],
        scratch_shapes=[pltpu.VMEM((HALF, 2 * LANES, LANES), F32)],
        compiler_params=pltpu.CompilerParams(vmem_limit_bytes=8 << 20),
        name="finish",
    )(rows, *centres)


def exchange(value):
    return lax.all_to_all(value, BOTH, 0, 0, tiled=True)


def swapped(value, mask):
    return lax.ppermute(value, "cent", [(i, i ^ mask) for i in range(16)])


def shifted(value, step):
    return lax.ppermute(value, "cent", [(i, (i + step) % 16) for i in range(16)])


def across(value):
    return lax.ppermute(value, BOTH, [(i, i ^ (4 * 16 + 2)) for i in range(128)])


def body(points, assign, counts, level2, l2_assign):
    assign = assign.reshape(-1, LANES)
    counts = counts.reshape(1, LANES)
    labels = l2_assign.reshape(1, LANES)
    sums = run_sums(points, assign, counts, labels, 0)
    near = jnp.concatenate([level2, across(level2)], axis=0)
    runs = exchange(sums)
    centres = jnp.concatenate([near] + [swapped(near, mask) for mask in (4, 8, 12)], axis=0)
    send, acc, rounds = means(runs)
    centres = [centres, swapped(centres, 1)]

    def more(state):
        index, _, acc = state
        sums = run_sums(points, assign, counts, labels, (index * SLOTS).reshape(1))
        send, acc, _ = means(exchange(sums), acc)
        return index + 1, send, acc

    _, send, _ = lax.while_loop(lambda state: state[0] < rounds[0], more, (jnp.int32(1), send, acc))
    new_level1, nearest, new_level2 = finish(exchange(send), centres)
    return new_level1, nearest.reshape(-1), new_level2


def solution(mesh):
    placed = (
        P(("dp", "cent"), None),
        P(("dp", "cent")),
        P("cent"),
        P("cent", None),
        P("cent", None),
    )
    return jax.shard_map(
        body,
        mesh=mesh,
        in_specs=placed,
        out_specs=(P("cent", None), P("cent"), P("cent", None)),
        check_vma=False,
    )
```
